32 devices in a mesh: group: 4 (over y, core), dev: 8 (over z, x).
Axes of the slice: x: 2, y: 2, z: 4, core: 2. Of those that a mesh axis runs over, the one named last changes fastest.
Arguments:
- points: float32 [440, 16384], P(None, ('group', 'dev')), may hold values from -6 to 6
- residual: float32 [147, 16384], P(None, ('group', 'dev')), may hold values from -6 to 6
- coeffs: float32 [147, 16384], P(None, ('group', 'dev')), may hold values from -3 to 3
- owners: int32 [2], replicated, may hold values from 0 to 31
- offsets: int32 [2], replicated, may hold values from 0 to 256
Outputs:
- new_residual: float32 [147, 16384], P(None, ('group', 'dev'))
- new_coeffs: float32 [147, 16384], P(None, ('group', 'dev'))
The draws below stay inside these ranges and needn't reach their ends.
All inputs are finite; a program needn't handle non-finite values.
Results may differ from the reference program's by a relative error of at most 0.0003.
Values sent between devices are 32-bit elements; how exact they have to be, the bound alone decides.
A program may use at most 64 MiB of HBM per device.

```python
import jax
import jax.numpy as jnp
from jax import lax

FEATURES = 440
CLASSES = 147
BLOCK = 256
ROWS_DEV = 512
NPTS = 16384
N_GROUP = 4
N_DEV = 8


def block_scale(key, dims, cuts, smallest, high):
    factor_of, own = 1.0, jax.random.fold_in(key, 6)
    for axis_at, shards_of in cuts:
        heights = jnp.exp(jax.random.uniform(jax.random.fold_in(own, axis_at), (shards_of,), jnp.float32, smallest / len(cuts), high / len(cuts)))
        factor_of = factor_of * jnp.repeat(heights, dims[axis_at] // shards_of).reshape([-1 if axis == axis_at else 1 for axis in range(len(dims))])
    return factor_of


def scatter_about(rng, shape, deviation, most, shards=(), kind=jnp.bfloat16):
    array = jax.random.normal(rng, shape, jnp.float32) * deviation
    if len(shards) > 0:
        array = block_scale(rng, shape, shards, -0.22, 0.18) * array
    return jnp.clip(array, min=-most, max=most).astype(kind)


def setup_inputs(seed: int = 0) -> dict:
    arg_keys = jax.random.split(jax.random.key(seed), 6)
    points = scatter_about(arg_keys[0], (FEATURES, NPTS), 1.0, 6.0, ((1, 32),), jnp.float32)
    residual = scatter_about(arg_keys[1], (CLASSES, NPTS), 1.0, 6.0, ((1, 32),), jnp.float32)
    coeffs = scatter_about(arg_keys[2], (CLASSES, NPTS), 0.5, 3.0, ((1, 32),), jnp.float32)
    owners = jax.random.randint(arg_keys[3], (2,), 0, N_GROUP * N_DEV).astype(jnp.int32)
    offsets = jax.random.randint(arg_keys[4], (2,), 0, ROWS_DEV - BLOCK + 1).astype(jnp.int32)
    return dict(points=points, residual=residual, coeffs=coeffs, owners=owners, offsets=offsets)


ridge = 2.0
step_norm = 1.5

def kernel_tile(cols, block):
    cross = lax.dot_general(block.astype(jnp.float32), cols.astype(jnp.float32), (((0,), (0,)), ((), ())), precision=lax.Precision.HIGHEST, preferred_element_type=jnp.float32)
    dist = lax.optimization_barrier(jnp.sum(block * block, axis=0))[:, None] + lax.optimization_barrier(jnp.sum(cols * cols, axis=0))[None, :] - 2.0 * cross
    return jnp.exp(-dist / cols.shape[0])

def precondition(grad, block):
    gram = kernel_tile(block, block) + ridge * jnp.eye(block.shape[1], dtype=jnp.float32)
    lower = jnp.linalg.cholesky(gram)
    inner = lax.linalg.triangular_solve(lower, grad.T, left_side=True, lower=True)
    solved = lax.linalg.triangular_solve(lower, inner, left_side=True, lower=True, transpose_a=True)
    scale = step_norm / jnp.sqrt(jnp.mean(grad * grad) + 1e-06)
    return scale * solved.T

def reference(points, residual, coeffs, owners, offsets):
    count = NPTS // ROWS_DEV
    for step in range(2):
        start = (owners[step] * ROWS_DEV + offsets[step]).astype(jnp.int32)
        block = lax.dynamic_slice_in_dim(points, start, BLOCK, 1)

        def accumulate(total, index):
            first = (index * ROWS_DEV).astype(jnp.int32)
            cols = lax.dynamic_slice_in_dim(points, first, ROWS_DEV, 1)
            resid = lax.dynamic_slice_in_dim(residual, first, ROWS_DEV, 1)
            tile = kernel_tile(cols, block)
            part = lax.dot_general(resid.astype(jnp.float32), tile.astype(jnp.float32), (((1,), (1,)), ((), ())), precision=lax.Precision.HIGHEST, preferred_element_type=jnp.float32)
            return (total + part, None)
        grad, _ = lax.scan(accumulate, jnp.zeros((CLASSES, BLOCK), jnp.float32), jnp.arange(count, dtype=jnp.int32))
        delta = precondition(grad, block)

        def update(index):
            first = (index * ROWS_DEV).astype(jnp.int32)
            cols = lax.dynamic_slice_in_dim(points, first, ROWS_DEV, 1)
            resid = lax.dynamic_slice_in_dim(residual, first, ROWS_DEV, 1)
            tile = kernel_tile(cols, block)
            return resid - jnp.dot(delta.astype(jnp.float32), tile.astype(jnp.float32), precision=lax.Precision.HIGHEST, preferred_element_type=jnp.float32)
        pieces = lax.map(update, jnp.arange(count, dtype=jnp.int32))
        residual = jnp.transpose(pieces, (1, 0, 2)).reshape(CLASSES, NPTS)
        current = lax.dynamic_slice_in_dim(coeffs, start, BLOCK, 1)
        coeffs = lax.dynamic_update_slice_in_dim(coeffs, current + delta, start, 1)
    return (residual, coeffs)
```

```python
import functools
import math

import jax
import jax.numpy as jnp
from jax import lax
from jax.experimental import pallas as pl
from jax.experimental.pallas import tpu as pltpu
from jax.sharding import PartitionSpec as P

BLOCK = 256
LANES = 128
SUB = 8
NEWTON_STEPS = 5

ridge = 2.0
step_norm = 1.5

MESH = pl.DeviceIdType.MESH
F32 = jnp.float32


def exact_dot(a, b, dims):
    return lax.dot_general(
        a, b, (dims, ((), ())), precision=lax.Precision.HIGHEST, preferred_element_type=F32
    )


NN = ((1,), (0,))
NT = ((1,), (1,))


def split_dot(a, b):
    ah, bh = a.astype(jnp.bfloat16), b.astype(jnp.bfloat16)
    al = (a - ah.astype(F32)).astype(jnp.bfloat16)
    bl = (b - bh.astype(F32)).astype(jnp.bfloat16)
    dot = functools.partial(jnp.dot, preferred_element_type=F32)
    return dot(ah, bh) + (dot(ah, bl) + dot(al, bh))


def factors(axis, size):
    if size > 2 and size % 2 == 0:
        return [(axis, 1, 2), (axis, 2, size // 2)]
    return [(axis, 1, size)]


def stage_orders(n_group, n_dev):
    group, dev = factors("group", n_group), factors("dev", n_dev)
    first = [group[0], dev[0]] + group[1:] + dev[1:]
    second = [group[0]] + group[1:] + [dev[0]] + dev[1:]
    return first, second


class Plan:
    def __init__(self, n_group, n_dev, features):
        n = n_group * n_dev
        tiles = 2 * (features // SUB) * (BLOCK // LANES)
        share = -(-tiles // n)
        self.tiles = share * n
        orders = stage_orders(n_group, n_dev)
        sizes = [(share + 1) // 2, share // 2]
        self.chunks = []
        start = 0
        self.copies = 0
        self.landing = 0
        for order, part in zip(orders, sizes):
            if part == 0:
                continue
            length = part * n
            stages = []
            now = length
            for axis, stride, size in order:
                piece = now // size
                stages.append((axis, stride, size, piece, self.landing, self.copies))
                self.landing += (size - 1) * piece
                self.copies += 2 * (size - 1)
                now = piece
            self.chunks.append((start, length, stages))
            start += length


def kernel(
    plan,
    n_group,
    n_dev,
    owners,
    offsets,
    points,
    residual,
    coeffs,
    new_residual,
    new_coeffs,
    buf,
    landed,
    blocks,
    padded,
    parts,
    arrived,
    sums,
    gram_inv,
    tiles,
    bsend,
    brecv,
    rsend,
    rrecv,
    gsend,
    grecv,
):
    n = n_group * n_dev
    group, dev = lax.axis_index("group"), lax.axis_index("dev")
    me = group * n_dev + dev
    features, here_points = points.shape
    classes = residual.shape[0]
    roots = padded.shape[0] // SUB
    per_block = (features // SUB) * (BLOCK // LANES)
    half = features // SUB

    def device(index):
        return (index // n_dev, lax.rem(index, n_dev))

    barrier = pltpu.get_barrier_semaphore()

    def greet(k, carry):
        pl.semaphore_signal(
            barrier, inc=1, device_id=device(lax.rem(me + k, n)), device_id_type=MESH
        )
        return carry

    lax.fori_loop(1, n, greet, 0)

    def picker(step):
        first = jnp.where(owners[step] == me, offsets[step], 4 * here_points)
        rows = lax.broadcasted_iota(jnp.int32, (BLOCK, here_points), 0)
        cols = lax.broadcasted_iota(jnp.int32, (BLOCK, here_points), 1)
        return jnp.where(cols == rows + first, 1.0, 0.0).astype(F32)

    for step in range(2):
        cand = exact_dot(points[...], picker(step), NT)
        at = step * per_block
        buf[at : at + half] = cand[:, :LANES].reshape(half, SUB, LANES)
        buf[at + half : at + 2 * half] = cand[:, LANES:].reshape(half, SUB, LANES)
    if plan.tiles > 2 * per_block:
        buf[2 * per_block :] = jnp.zeros((plan.tiles - 2 * per_block, SUB, LANES), F32)

    padded[...] = jnp.zeros_like(padded)
    padded[:classes] = residual[...]

    pl.semaphore_wait(barrier, n - 1)

    def position(stage):
        axis, stride, size = stage[:3]
        at = group if axis == "group" else dev
        return lax.rem(at // stride, size)

    def partner(stage, index):
        axis, stride = stage[:2]
        shift = (index - position(stage)) * stride
        return (group + shift, dev) if axis == "group" else (group, dev + shift)

    offs = [start for start, _, _ in plan.chunks]
    steps = len(plan.chunks[0][2])
    started = []
    for s in range(steps):
        copies = []
        for c, (_, _, stages) in enumerate(plan.chunks):
            stage = stages[s]
            size, piece, base, sem = stage[2:]
            mine = position(stage)
            for k in range(1, size):
                to = lax.rem(mine + k, size)
                copy = pltpu.make_async_remote_copy(
                    src_ref=buf.at[pl.ds(offs[c] + to * piece, piece)],
                    dst_ref=landed.at[pl.ds(base + (k - 1) * piece, piece)],
                    send_sem=bsend.at[sem + k - 1],
                    recv_sem=brecv.at[sem + k - 1],
                    device_id=partner(stage, to),
                    device_id_type=MESH,
                )
                copy.start()
                copies.append(copy)
        for copy in copies:
            copy.wait_recv()
        started += copies
        for c, (_, _, stages) in enumerate(plan.chunks):
            stage = stages[s]
            size, piece, base, sem = stage[2:]
            offs[c] = offs[c] + position(stage) * piece
            total = buf[pl.ds(offs[c], piece)]
            for k in range(1, size):
                total = total + landed[base + (k - 1) * piece : base + k * piece]
            if s == steps - 1:
                blocks[pl.ds(offs[c], piece)] = total
            else:
                buf[pl.ds(offs[c], piece)] = total
    for s in reversed(range(steps)):
        copies = []
        for c, (_, _, stages) in enumerate(plan.chunks):
            stage = stages[s]
            size, piece, base, sem = stage[2:]
            mine = position(stage)
            for k in range(1, size):
                to = lax.rem(mine + k, size)
                where = blocks.at[pl.ds(offs[c], piece)]
                copy = pltpu.make_async_remote_copy(
                    src_ref=where,
                    dst_ref=where,
                    send_sem=bsend.at[sem + size - 1 + k - 1],
                    recv_sem=brecv.at[sem + size - 1 + k - 1],
                    device_id=partner(stage, to),
                    device_id_type=MESH,
                )
                copy.start()
                copies.append(copy)
            offs[c] = offs[c] - mine * piece
        for copy in copies:
            copy.wait_recv()
        started += copies

    cols = points[...]
    cols_norm = jnp.sum(cols * cols, axis=0, keepdims=True)

    def block(step):
        at = step * per_block
        left = blocks[at : at + half].reshape(features, LANES)
        right = blocks[at + half : at + 2 * half].reshape(features, LANES)
        return jnp.concatenate([left, right], axis=1)

    def kernel_tile(flipped, others, others_norm):
        cross = exact_dot(flipped, others, NN)
        norm = jnp.sum(flipped * flipped, axis=1, keepdims=True)
        return jnp.exp(-(norm + others_norm - 2.0 * cross) / features)

    def make_tile(step):
        tiles[step] = kernel_tile(block(step).T, cols, cols_norm)

    eye = (
        lax.broadcasted_iota(jnp.int32, (BLOCK, BLOCK), 0)
        == lax.broadcasted_iota(jnp.int32, (BLOCK, BLOCK), 1)
    ).astype(F32)

    def make_inverse(step):
        b = block(step)
        gram = kernel_tile(b.T, b, jnp.sum(b * b, axis=0, keepdims=True)) + ridge * eye
        gram_inv[step, 0] = gram
        top = jnp.max(jnp.sum(gram, axis=1, keepdims=True), axis=0, keepdims=True)
        centre = 2.0 / (ridge + top)
        err = (top - ridge) / (top + ridge)
        gain = 2.0 / (2.0 - err * err)
        inv = (gain * centre) * (2.0 * eye - centre * gram)
        err = err * err / (2.0 - err * err)
        for _ in range(NEWTON_STEPS):
            gain = 2.0 / (2.0 - err * err)
            inv = gain * split_dot(inv, 2.0 * eye - split_dot(gram, inv))
            err = err * err / (2.0 - err * err)
        gram_inv[step, 1] = inv

    def scatter_copy(step, k):
        to = lax.rem(me + k, n)
        return to, pltpu.make_async_remote_copy(
            src_ref=parts.at[step, jnp.minimum(to, roots - 1)],
            dst_ref=arrived.at[step, k - 1],
            send_sem=rsend.at[step, k - 1],
            recv_sem=rrecv.at[step, k - 1],
            device_id=device(to),
            device_id_type=MESH,
        )

    def gather_copy(step, k, root):
        return pltpu.make_async_remote_copy(
            src_ref=sums.at[step, root],
            dst_ref=sums.at[step, root],
            send_sem=gsend.at[step, k - 1],
            recv_sem=grecv.at[step, root],
            device_id=device(lax.rem(me + k, n)),
            device_id_type=MESH,
        )

    mine = jnp.minimum(me, roots - 1)

    def loop(first, last, body):
        def run(k, carry):
            body(k)
            return carry

        lax.fori_loop(first, last, run, 0)

    def sum_start(step):
        part = exact_dot(padded[...], tiles[step], NT)
        parts[step] = part.reshape(roots, SUB, BLOCK)

        def send(k):
            to, copy = scatter_copy(step, k)
            pl.when(to < roots)(copy.start)

        loop(1, n, send)

    def sum_reduce(step):
        @pl.when(me < roots)
        def _():
            loop(1, n, lambda k: scatter_copy(step, k)[1].wait_recv())
            sums[step, mine] = parts[step, mine] + jnp.sum(arrived[step], axis=0)
            loop(1, n, lambda k: gather_copy(step, k, mine).start())

    def sum_finish(step):
        def receive(root):
            @pl.when(root != me)
            def _():
                gather_copy(step, 1, root).wait_recv()

        loop(0, roots, receive)
        return sums[step].reshape(roots * SUB, BLOCK)

    def sum_settle(step):
        def settle(k):
            to, copy = scatter_copy(step, k)
            pl.when(to < roots)(copy.wait_send)

        loop(1, n, settle)

        @pl.when(me < roots)
        def _():
            loop(1, n, lambda k: gather_copy(step, k, mine).wait_send())

    def precondition(step, grad):
        gram, inv = gram_inv[step, 0], gram_inv[step, 1]
        guess = exact_dot(grad, inv, NN)
        solved = guess + exact_dot(grad - exact_dot(guess, gram, NN), inv, NN)
        square = jnp.sum(jnp.sum(grad * grad, axis=1, keepdims=True), axis=0, keepdims=True)
        return step_norm / jnp.sqrt(square / (classes * BLOCK) + 1e-06) * solved

    make_tile(0)
    sum_start(0)
    make_tile(1)
    sum_reduce(0)
    make_inverse(0)
    delta = precondition(0, sum_finish(0))
    padded[...] = padded[...] - exact_dot(delta, tiles[0], NN)
    sum_start(1)
    new_coeffs[...] = coeffs[...] + exact_dot(delta, picker(0), NN)[:classes]
    sum_reduce(1)
    make_inverse(1)
    delta = precondition(1, sum_finish(1))
    new_residual[...] = (padded[...] - exact_dot(delta, tiles[1], NN))[:classes]
    new_coeffs[...] = new_coeffs[...] + exact_dot(delta, picker(1), NN)[:classes]
    for copy in started:
        copy.wait_send()
    sum_settle(0)
    sum_settle(1)


def solution(mesh):
    n_group, n_dev = mesh.shape["group"], mesh.shape["dev"]
    n = n_group * n_dev

    def body(points, residual, coeffs, owners, offsets):
        features, here = points.shape
        classes = residual.shape[0]
        plan = Plan(n_group, n_dev, features)
        roots = -(-classes // SUB)
        vmem = pl.BlockSpec(memory_space=pltpu.VMEM)
        smem = pl.BlockSpec(memory_space=pltpu.SMEM)
        dma = pltpu.SemaphoreType.DMA
        return pl.pallas_call(
            functools.partial(kernel, plan, n_group, n_dev),
            out_shape=(
                jax.ShapeDtypeStruct(residual.shape, F32),
                jax.ShapeDtypeStruct(coeffs.shape, F32),
            ),
            in_specs=[smem, smem, vmem, vmem, vmem],
            out_specs=(vmem, vmem),
            scratch_shapes=[
                pltpu.VMEM((plan.tiles, SUB, LANES), F32),
                pltpu.VMEM((plan.landing, SUB, LANES), F32),
                pltpu.VMEM((plan.tiles, SUB, LANES), F32),
                pltpu.VMEM((roots * SUB, here), F32),
                pltpu.VMEM((2, roots, SUB, BLOCK), F32),
                pltpu.VMEM((2, n - 1, SUB, BLOCK), F32),
                pltpu.VMEM((2, roots, SUB, BLOCK), F32),
                pltpu.VMEM((2, 2, BLOCK, BLOCK), F32),
                pltpu.VMEM((2, BLOCK, here), F32),
                dma((plan.copies,)),
                dma((plan.copies,)),
                dma((2, n - 1)),
                dma((2, n - 1)),
                dma((2, n - 1)),
                dma((2, roots)),
            ],
            compiler_params=pltpu.CompilerParams(
                collective_id=0, has_side_effects=True, vmem_limit_bytes=40 * 1024 * 1024
            ),
        )(owners, offsets, points, residual, coeffs)

    split = P(None, ("group", "dev"))
    return jax.shard_map(
        body,
        mesh=mesh,
        in_specs=(split, split, split, P(), P()),
        out_specs=(split, split),
        check_vma=False,
    )
```

```python
import functools

import jax
import jax.numpy as jnp
from jax import lax
from jax.experimental import pallas as pl
from jax.experimental.pallas import tpu as pltpu
from jax.sharding import PartitionSpec as P

BLOCK = 256
LANES = 128
SUB = 8
NEWTON_STEPS = 5

ridge = 2.0
step_norm = 1.5

MESH = pl.DeviceIdType.MESH
F32 = jnp.float32


def exact_dot(a, b, dims):
    return lax.dot_general(
        a, b, (dims, ((), ())), precision=lax.Precision.HIGHEST, preferred_element_type=F32
    )


NN = ((1,), (0,))
NT = ((1,), (1,))


def split_dot(a, b):
    ah, bh = a.astype(jnp.bfloat16), b.astype(jnp.bfloat16)
    al = (a - ah.astype(F32)).astype(jnp.bfloat16)
    bl = (b - bh.astype(F32)).astype(jnp.bfloat16)
    dot = functools.partial(jnp.dot, preferred_element_type=F32)
    return dot(ah, bh) + (dot(ah, bl) + dot(al, bh))


def split_three(x):
    high = x.astype(jnp.bfloat16)
    rest = x - high.astype(F32)
    mid = rest.astype(jnp.bfloat16)
    return high, mid, (rest - mid.astype(F32)).astype(jnp.bfloat16)


def line_width(n_dev):
    width = 1
    while n_dev % (2 * width) == 0 and 4 * width * width <= n_dev:
        width *= 2
    return width


class Layout:
    def __init__(self, n_group, n_dev):
        self.n_dev = n_dev
        self.width = line_width(n_dev)
        self.plane = n_group * self.width
        self.line = n_dev // self.width

    def share(self, tiles):
        return -(-tiles // self.plane)


class Sum:
    def __init__(self, layout, at, share, refs):
        self.layout, self.share = layout, share
        self.group, self.dev = at
        self.terms, self.landed, self.held, self.crossed, self.total, self.sems = refs
        self.place = self.group * layout.width + lax.rem(self.dev, layout.width)
        self.plane = self.dev // layout.width
        self.started = []

    def peer_in_plane(self, k):
        to = lax.rem(self.place + k, self.layout.plane)
        width = self.layout.width
        return to, (to // width, self.plane * width + lax.rem(to, width))

    def peer_in_line(self, k):
        to = lax.rem(self.plane + k, self.layout.line)
        width = self.layout.width
        return self.group, to * width + lax.rem(self.dev, width)

    def piece(self, index):
        return pl.ds(index * self.share, self.share)

    def send(self, src, dst, sem, to):
        copy = pltpu.make_async_remote_copy(
            src_ref=src,
            dst_ref=dst,
            send_sem=self.sems.at[0, sem],
            recv_sem=self.sems.at[1, sem],
            device_id=to,
            device_id_type=MESH,
        )
        copy.start()
        self.waiting.append(copy)

    def arrive(self):
        for copy in self.waiting:
            copy.wait_recv()
        self.started += self.waiting

    def scatter(self):
        self.waiting = []
        for k in range(1, self.layout.plane):
            to, device = self.peer_in_plane(k)
            self.send(self.terms.at[self.piece(to)], self.landed.at[self.piece(k - 1)], k - 1, device)

    def cross(self):
        self.arrive()
        total = self.terms[self.piece(self.place)]
        for k in range(self.layout.plane - 1):
            total = total + self.landed[self.piece(k)]
        self.held[...] = total
        self.waiting = []
        first = self.layout.plane - 1
        for k in range(1, self.layout.line):
            self.send(self.held, self.crossed.at[self.piece(k - 1)], first + k - 1, self.peer_in_line(k))

    def gather(self):
        self.arrive()
        total = self.held[...]
        for k in range(self.layout.line - 1):
            total = total + self.crossed[self.piece(k)]
        mine = self.total.at[self.piece(self.place)]
        mine[...] = total
        self.waiting = []
        first = self.layout.plane + self.layout.line - 2
        for k in range(1, self.layout.plane):
            self.send(mine, mine, first + k - 1, self.peer_in_plane(k)[1])

    def finish(self):
        self.arrive()

    def settle(self):
        for copy in self.started:
            copy.wait_send()


def sum_scratch(layout, share):
    tile = (SUB, LANES)
    copies = 2 * (layout.plane - 1) + layout.line - 1
    return [
        pltpu.VMEM((layout.plane * share,) + tile, F32),
        pltpu.VMEM((max(layout.plane - 1, 1) * share,) + tile, F32),
        pltpu.VMEM((share,) + tile, F32),
        pltpu.VMEM((max(layout.line - 1, 1) * share,) + tile, F32),
        pltpu.VMEM((layout.plane * share,) + tile, F32),
        pltpu.SemaphoreType.DMA((2, copies)),
    ]


def to_tiles(ref, value):
    rows, columns = value.shape
    half = rows // SUB
    for c in range(columns // LANES):
        ref[c * half : (c + 1) * half] = value[:, c * LANES : (c + 1) * LANES].reshape(half, SUB, LANES)
    left = ref.shape[0] - half * (columns // LANES)
    if left:
        ref[ref.shape[0] - left :] = jnp.zeros((left, SUB, LANES), F32)


def from_tiles(ref, rows, columns):
    half = rows // SUB
    return jnp.concatenate(
        [ref[c * half : (c + 1) * half].reshape(rows, LANES) for c in range(columns // LANES)], axis=1
    )


def kernel(layout, n_group, owners_in, offsets_in, points_in, residual_in, coeffs_in, new_residual, new_coeffs, *scratch):
    owners, offsets, points, residual, coeffs, padded, flipped, tiles, grams, loads = scratch[:10]
    sums = [scratch[10 + 6 * i : 16 + 6 * i] for i in range(4)]
    group, dev = lax.axis_index("group"), lax.axis_index("dev")
    me = group * layout.n_dev + dev
    features, here_points = points.shape
    classes = residual.shape[0]
    rows = padded.shape[0]

    copies = [
        pltpu.make_async_copy(src, dst, loads.at[i])
        for i, (src, dst) in enumerate(
            [(points_in, points), (owners_in, owners), (offsets_in, offsets), (residual_in, residual), (coeffs_in, coeffs)]
        )
    ]
    for copy in copies:
        copy.start()

    blocks_share = sums[0][2].shape[0]
    grads_share = sums[2][2].shape[0]
    spread = [Sum(layout, (group, dev), blocks_share, sums[i]) for i in range(2)]
    grads = [Sum(layout, (group, dev), grads_share, sums[2 + i]) for i in range(2)]

    barrier = pltpu.get_barrier_semaphore()
    peers = [spread[0].peer_in_plane(k)[1] for k in range(1, layout.plane)]
    peers += [spread[0].peer_in_line(k) for k in range(1, layout.line)]
    for peer in peers:
        pl.semaphore_signal(barrier, inc=1, device_id=peer, device_id_type=MESH)

    def picker(step):
        first = jnp.where(owners[step] == me, offsets[step], 4 * here_points)
        row = lax.broadcasted_iota(jnp.int32, (BLOCK, here_points), 0)
        col = lax.broadcasted_iota(jnp.int32, (BLOCK, here_points), 1)
        return jnp.where(col == row + first, 1.0, 0.0).astype(jnp.bfloat16)

    def pick(step, pieces):
        chosen = picker(step)
        dot = lambda a: lax.dot_general(a, chosen, (NT, ((), ())), preferred_element_type=F32)
        high, mid, low = pieces
        to_tiles(spread[step].terms, (dot(high) + dot(mid)) + dot(low))

    for copy in copies[:3]:
        copy.wait()
    pieces = split_three(points[...])
    pick(0, pieces)
    pl.semaphore_wait(barrier, len(peers))
    spread[0].scatter()
    pick(1, pieces)

    cols = points[...].T
    flipped[...] = cols
    cols_norm = jnp.sum(cols * cols, axis=1, keepdims=True)
    for copy in copies[3:]:
        copy.wait()
    padded[...] = jnp.zeros_like(padded)
    padded[:classes] = residual[...]

    spread[0].cross()
    spread[1].scatter()
    spread[0].gather()
    spread[1].cross()
    spread[0].finish()

    eye = (
        lax.broadcasted_iota(jnp.int32, (BLOCK, BLOCK), 0)
        == lax.broadcasted_iota(jnp.int32, (BLOCK, BLOCK), 1)
    ).astype(F32)

    def kernel_tile(left, left_norm, right):
        cross = exact_dot(left, right, NN)
        right_norm = jnp.sum(right * right, axis=0, keepdims=True)
        return jnp.exp(-(left_norm + right_norm - 2.0 * cross) / features)

    def block(step):
        return from_tiles(spread[step].total, features, BLOCK)

    def make_tile(step):
        tiles[step] = kernel_tile(flipped[...], cols_norm, block(step))

    class Inverse:
        def __init__(self, step):
            b = block(step)
            bt = b.T
            gram = kernel_tile(bt, jnp.sum(bt * bt, axis=1, keepdims=True), b) + ridge * eye
            top = jnp.max(jnp.sum(gram, axis=1, keepdims=True), axis=0, keepdims=True)
            centre = 2.0 / (ridge + top)
            err = (top - ridge) / (top + ridge)
            gain = 2.0 / (2.0 - err * err)
            self.gram = gram
            self.value = (gain * centre) * (2.0 * eye - centre * gram)
            self.err = err * err / (2.0 - err * err)

        def improve(self, times):
            for _ in range(times):
                err = self.err
                gain = 2.0 / (2.0 - err * err)
                self.value = gain * split_dot(self.value, 2.0 * eye - split_dot(self.gram, self.value))
                self.err = err * err / (2.0 - err * err)

        def polish(self):
            rest = eye - exact_dot(self.gram, self.value, NN)
            return self.value + exact_dot(self.value, rest, NN)

    def sum_grad(step):
        to_tiles(grads[step].terms, exact_dot(padded[...], tiles[step], NN))
        grads[step].scatter()

    def make_delta(step, inverse):
        grad = from_tiles(grads[step].total, rows, BLOCK)
        square = jnp.sum(jnp.sum(grad * grad, axis=1, keepdims=True), axis=0, keepdims=True)
        scale = step_norm / jnp.sqrt(square / (classes * BLOCK) + 1e-06)
        return scale * exact_dot(grad, inverse, NN)

    def credit(step, delta):
        chosen = picker(step)
        high, mid, low = split_three(delta)
        dot = lambda a: jnp.dot(a, chosen, preferred_element_type=F32)
        return ((dot(high) + dot(mid)) + dot(low))[:classes]

    make_tile(0)
    sum_grad(0)
    spread[1].gather()
    inverse = Inverse(0)
    inverse.improve(1)
    grads[0].cross()
    inverse.improve(NEWTON_STEPS - 1)
    grads[0].gather()
    inverse = inverse.polish()
    spread[1].finish()
    make_tile(1)
    grads[0].finish()
    delta = make_delta(0, inverse)
    padded[...] = padded[...] - exact_dot(delta, tiles[0], NT)
    sum_grad(1)
    new_coeffs[...] = coeffs[...] + credit(0, delta)
    inverse = Inverse(1)
    inverse.improve(1)
    grads[1].cross()
    inverse.improve(NEWTON_STEPS - 1)
    grads[1].gather()
    inverse = inverse.polish()
    grads[1].finish()
    delta = make_delta(1, inverse)
    new_residual[...] = (padded[...] - exact_dot(delta, tiles[1], NT))[:classes]
    new_coeffs[...] = new_coeffs[...] + credit(1, delta)
    for each in spread + grads:
        each.settle()


def solution(mesh):
    n_group, n_dev = mesh.shape["group"], mesh.shape["dev"]
    layout = Layout(n_group, n_dev)

    def body(points, residual, coeffs, owners, offsets):
        features, here = points.shape
        classes = residual.shape[0]
        rows = -(-classes // SUB) * SUB
        columns = BLOCK // LANES
        blocks_share = layout.share(features // SUB * columns)
        grads_share = layout.share(rows // SUB * columns)
        vmem = pl.BlockSpec(memory_space=pltpu.VMEM)
        anywhere = pl.BlockSpec(memory_space=pl.ANY)
        return pl.pallas_call(
            functools.partial(kernel, layout, n_group),
            out_shape=(
                jax.ShapeDtypeStruct(residual.shape, F32),
                jax.ShapeDtypeStruct(coeffs.shape, F32),
            ),
            in_specs=[anywhere] * 5,
            out_specs=(vmem, vmem),
            scratch_shapes=[
                pltpu.SMEM(owners.shape, jnp.int32),
                pltpu.SMEM(offsets.shape, jnp.int32),
                pltpu.VMEM(points.shape, F32),
                pltpu.VMEM(residual.shape, F32),
                pltpu.VMEM(coeffs.shape, F32),
                pltpu.VMEM((rows, here), F32),
                pltpu.VMEM((here, features), F32),
                pltpu.VMEM((2, here, BLOCK), F32),
                pltpu.VMEM((2, BLOCK, BLOCK), F32),
                pltpu.SemaphoreType.DMA((5,)),
            ]
            + sum_scratch(layout, blocks_share) * 2
            + sum_scratch(layout, grads_share) * 2,
            compiler_params=pltpu.CompilerParams(
                collective_id=0, has_side_effects=True, vmem_limit_bytes=60 * 1024 * 1024
            ),
        )(owners, offsets, points, residual, coeffs)

    split = P(None, ("group", "dev"))
    return jax.shard_map(
        body,
        mesh=mesh,
        in_specs=(split, split, split, P(), P()),
        out_specs=(split, split),
        check_vma=False,
    )
```

```python
import functools

import jax
import jax.numpy as jnp
from jax import lax
from jax.experimental import pallas as pl
from jax.experimental.pallas import tpu as pltpu
from jax.sharding import PartitionSpec as P

BLOCK = 256
LANES = 128
SUB = 8

ridge = 2.0
step_norm = 1.5

MESH = pl.DeviceIdType.MESH
F32 = jnp.float32


def exact_dot(a, b, dims):
    return lax.dot_general(
        a, b, (dims, ((), ())), precision=lax.Precision.HIGHEST, preferred_element_type=F32
    )


NN = ((1,), (0,))
NT = ((1,), (1,))


def low_dot(a, b):
    return jnp.dot(a.astype(jnp.bfloat16), b.astype(jnp.bfloat16), preferred_element_type=F32)


def split_dot(a, b, dims=NN):
    ah, bh = a.astype(jnp.bfloat16), b.astype(jnp.bfloat16)
    al = (a - ah.astype(F32)).astype(jnp.bfloat16)
    bl = (b - bh.astype(F32)).astype(jnp.bfloat16)
    dot = lambda u, v: lax.dot_general(u, v, (dims, ((), ())), preferred_element_type=F32)
    return dot(ah, bh) + (dot(ah, bl) + dot(al, bh))


def split_three(x):
    high = x.astype(jnp.bfloat16)
    rest = x - high.astype(F32)
    mid = rest.astype(jnp.bfloat16)
    return high, mid, (rest - mid.astype(F32)).astype(jnp.bfloat16)


def line_width(n_dev):
    width = 1
    while n_dev % (2 * width) == 0 and 4 * width * width <= n_dev:
        width *= 2
    return width


class Layout:
    def __init__(self, n_group, n_dev):
        self.n_dev = n_dev
        self.width = line_width(n_dev)
        self.plane = n_group * self.width
        self.line = n_dev // self.width

    def share(self, tiles):
        return -(-tiles // self.plane)


class Sum:
    def __init__(self, layout, at, share, refs):
        self.layout, self.share = layout, share
        self.group, self.dev = at
        self.terms, self.landed, self.held, self.crossed, self.total, self.sems = refs
        self.place = self.group * layout.width + lax.rem(self.dev, layout.width)
        self.plane = self.dev // layout.width
        self.started = []

    def peer_in_plane(self, k):
        to = lax.rem(self.place + k, self.layout.plane)
        width = self.layout.width
        return to, (to // width, self.plane * width + lax.rem(to, width))

    def peer_in_line(self, k):
        to = lax.rem(self.plane + k, self.layout.line)
        width = self.layout.width
        return self.group, to * width + lax.rem(self.dev, width)

    def piece(self, index):
        return pl.ds(index * self.share, self.share)

    def send(self, src, dst, sem, to):
        copy = pltpu.make_async_remote_copy(
            src_ref=src,
            dst_ref=dst,
            send_sem=self.sems.at[0, sem],
            recv_sem=self.sems.at[1, sem],
            device_id=to,
            device_id_type=MESH,
        )
        copy.start()
        self.waiting.append(copy)

    def arrive(self):
        for copy in self.waiting:
            copy.wait_recv()
        self.started += self.waiting

    def scatter(self):
        self.waiting = []
        for k in range(1, self.layout.plane):
            to, device = self.peer_in_plane(k)
            self.send(self.terms.at[self.piece(to)], self.landed.at[self.piece(k - 1)], k - 1, device)

    def cross(self):
        self.arrive()
        total = self.terms[self.piece(self.place)]
        for k in range(self.layout.plane - 1):
            total = total + self.landed[self.piece(k)]
        self.held[...] = total
        self.waiting = []
        first = self.layout.plane - 1
        for k in range(1, self.layout.line):
            self.send(self.held, self.crossed.at[self.piece(k - 1)], first + k - 1, self.peer_in_line(k))

    def gather(self):
        self.arrive()
        total = self.held[...]
        for k in range(self.layout.line - 1):
            total = total + self.crossed[self.piece(k)]
        mine = self.total.at[self.piece(self.place)]
        mine[...] = total
        self.waiting = []
        first = self.layout.plane + self.layout.line - 2
        for k in range(1, self.layout.plane):
            self.send(mine, mine, first + k - 1, self.peer_in_plane(k)[1])

    def finish(self):
        self.arrive()

    def settle(self):
        for copy in self.started:
            copy.wait_send()


def sum_scratch(layout, share):
    tile = (SUB, LANES)
    copies = 2 * (layout.plane - 1) + layout.line - 1
    return [
        pltpu.VMEM((layout.plane * share,) + tile, F32),
        pltpu.VMEM((max(layout.plane - 1, 1) * share,) + tile, F32),
        pltpu.VMEM((share,) + tile, F32),
        pltpu.VMEM((max(layout.line - 1, 1) * share,) + tile, F32),
        pltpu.VMEM((layout.plane * share,) + tile, F32),
        pltpu.SemaphoreType.DMA((2, copies)),
    ]


def to_tiles(ref, value):
    rows, columns = value.shape
    half = rows // SUB
    for c in range(columns // LANES):
        ref[c * half : (c + 1) * half] = value[:, c * LANES : (c + 1) * LANES].reshape(half, SUB, LANES)
    left = ref.shape[0] - half * (columns // LANES)
    if left:
        ref[ref.shape[0] - left :] = jnp.zeros((left, SUB, LANES), F32)


def from_tiles(ref, rows, columns):
    half = rows // SUB
    return jnp.concatenate(
        [ref[c * half : (c + 1) * half].reshape(rows, LANES) for c in range(columns // LANES)], axis=1
    )


def kernel(layout, n_group, owners_in, offsets_in, points_in, residual_in, change_residual, change_coeffs, *scratch):
    owners, offsets, points, residual, padded, flipped, tiles, loads = scratch[:8]
    sums = [scratch[8 + 6 * i : 14 + 6 * i] for i in range(4)]
    group, dev = lax.axis_index("group"), lax.axis_index("dev")
    me = group * layout.n_dev + dev
    features, here_points = points.shape
    classes = residual.shape[0]
    rows = padded.shape[0]

    copies = [
        pltpu.make_async_copy(src, dst, loads.at[i])
        for i, (src, dst) in enumerate(
            [(points_in, points), (owners_in, owners), (offsets_in, offsets), (residual_in, residual)]
        )
    ]
    for copy in copies:
        copy.start()

    blocks_share = sums[0][2].shape[0]
    grads_share = sums[2][2].shape[0]
    spread = [Sum(layout, (group, dev), blocks_share, sums[i]) for i in range(2)]
    grads = [Sum(layout, (group, dev), grads_share, sums[2 + i]) for i in range(2)]

    barrier = pltpu.get_barrier_semaphore()
    peers = [spread[0].peer_in_plane(k)[1] for k in range(1, layout.plane)]
    peers += [spread[0].peer_in_line(k) for k in range(1, layout.line)]
    for peer in peers:
        pl.semaphore_signal(barrier, inc=1, device_id=peer, device_id_type=MESH)

    def picker(step):
        first = jnp.where(owners[step] == me, offsets[step], 4 * here_points)
        row = lax.broadcasted_iota(jnp.int32, (BLOCK, here_points), 0)
        col = lax.broadcasted_iota(jnp.int32, (BLOCK, here_points), 1)
        return jnp.where(col == row + first, 1.0, 0.0).astype(jnp.bfloat16)

    def pick(step, pieces):
        chosen = picker(step)
        dot = lambda a: lax.dot_general(a, chosen, (NT, ((), ())), preferred_element_type=F32)
        high, mid, low = pieces
        to_tiles(spread[step].terms, (dot(high) + dot(mid)) + dot(low))

    for copy in copies[:3]:
        copy.wait()
    pieces = split_three(points[...])
    pick(0, pieces)
    pl.semaphore_wait(barrier, len(peers))
    spread[0].scatter()
    pick(1, pieces)

    cols = points[...].T
    flipped[...] = cols
    cols_norm = jnp.sum(cols * cols, axis=1, keepdims=True)
    for copy in copies[3:]:
        copy.wait()
    padded[...] = jnp.zeros_like(padded)
    padded[:classes] = residual[...]

    spread[0].cross()
    spread[1].scatter()
    spread[0].gather()
    spread[1].cross()
    spread[0].finish()

    eye = (
        lax.broadcasted_iota(jnp.int32, (BLOCK, BLOCK), 0)
        == lax.broadcasted_iota(jnp.int32, (BLOCK, BLOCK), 1)
    ).astype(F32)

    def kernel_tile(left, left_norm, right):
        cross = exact_dot(left, right, NN)
        right_norm = jnp.sum(right * right, axis=0, keepdims=True)
        return jnp.exp(-(left_norm + right_norm - 2.0 * cross) / features)

    def block(step):
        return from_tiles(spread[step].total, features, BLOCK)

    def make_tile(step):
        tiles[step] = kernel_tile(flipped[...], cols_norm, block(step))

    class Inverse:
        def __init__(self, step):
            b = block(step)
            bt = b.T
            gram = kernel_tile(bt, jnp.sum(bt * bt, axis=1, keepdims=True), b) + ridge * eye
            top = jnp.max(jnp.sum(gram, axis=1, keepdims=True), axis=0, keepdims=True)
            centre = 2.0 / (ridge + top)
            err = (top - ridge) / (top + ridge)
            gain = 2.0 / (2.0 - err * err)
            self.gram = gram
            self.value = (gain * centre) * (2.0 * eye - centre * gram)
            self.err = err * err / (2.0 - err * err)

        def gain(self):
            err = self.err
            self.err = err * err / (2.0 - err * err)
            return 2.0 / (2.0 - err * err)

        def rough(self):
            near = self.value.astype(jnp.bfloat16)
            rest = eye - low_dot(self.gram, near)
            self.value = self.gain() * (near.astype(F32) + low_dot(near, rest))

        def fine(self):
            rest = eye - split_dot(self.gram, self.value)
            self.value = self.gain() * (self.value + low_dot(self.value, rest))

        def polish(self):
            rest = eye - exact_dot(self.gram, self.value, NN)
            self.value = self.value + low_dot(self.value, rest)

    def sum_grad(step):
        to_tiles(grads[step].terms, exact_dot(padded[...], tiles[step], NN))
        grads[step].scatter()

    def make_delta(step, inverse):
        grad = from_tiles(grads[step].total, rows, BLOCK)
        square = jnp.sum(jnp.sum(grad * grad, axis=1, keepdims=True), axis=0, keepdims=True)
        scale = step_norm / jnp.sqrt(square / (classes * BLOCK) + 1e-06)
        return scale * exact_dot(grad, inverse, NN)

    def credit(step, delta):
        chosen = picker(step)
        high, mid, low = split_three(delta)
        dot = lambda a: jnp.dot(a, chosen, preferred_element_type=F32)
        return ((dot(high) + dot(mid)) + dot(low))[:classes]

    make_tile(0)
    sum_grad(0)
    spread[1].gather()
    inverse = Inverse(0)
    inverse.rough()
    grads[0].cross()
    inverse.rough()
    inverse.rough()
    inverse.fine()
    grads[0].gather()
    inverse.fine()
    inverse.polish()
    spread[1].finish()
    make_tile(1)
    grads[0].finish()
    delta = make_delta(0, inverse.value)
    change = split_dot(delta, tiles[0], NT)
    padded[...] = padded[...] - change
    sum_grad(1)
    change_residual[...] = change[:classes]
    change_coeffs[...] = credit(0, delta)
    inverse = Inverse(1)
    inverse.rough()
    grads[1].cross()
    inverse.rough()
    inverse.rough()
    inverse.fine()
    grads[1].gather()
    inverse.fine()
    inverse.polish()
    grads[1].finish()
    delta = make_delta(1, inverse.value)
    change_residual[...] = change_residual[...] + split_dot(delta, tiles[1], NT)[:classes]
    change_coeffs[...] = change_coeffs[...] + credit(1, delta)
    for each in spread + grads:
        each.settle()


def solution(mesh):
    n_group, n_dev = mesh.shape["group"], mesh.shape["dev"]
    layout = Layout(n_group, n_dev)

    def body(points, residual, coeffs, owners, offsets):
        features, here = points.shape
        classes = residual.shape[0]
        rows = -(-classes // SUB) * SUB
        columns = BLOCK // LANES
        blocks_share = layout.share(features // SUB * columns)
        grads_share = layout.share(rows // SUB * columns)
        vmem = pl.BlockSpec(memory_space=pltpu.VMEM)
        anywhere = pl.BlockSpec(memory_space=pl.ANY)
        change_residual, change_coeffs = pl.pallas_call(
            functools.partial(kernel, layout, n_group),
            out_shape=(
                jax.ShapeDtypeStruct(residual.shape, F32),
                jax.ShapeDtypeStruct(coeffs.shape, F32),
            ),
            in_specs=[anywhere] * 4,
            out_specs=(vmem, vmem),
            scratch_shapes=[
                pltpu.SMEM(owners.shape, jnp.int32),
                pltpu.SMEM(offsets.shape, jnp.int32),
                pltpu.VMEM(points.shape, F32),
                pltpu.VMEM(residual.shape, F32),
                pltpu.VMEM((rows, here), F32),
                pltpu.VMEM((here, features), F32),
                pltpu.VMEM((2, here, BLOCK), F32),
                pltpu.SemaphoreType.DMA((4,)),
            ]
            + sum_scratch(layout, blocks_share) * 2
            + sum_scratch(layout, grads_share) * 2,
            compiler_params=pltpu.CompilerParams(
                collective_id=0, has_side_effects=True, vmem_limit_bytes=60 * 1024 * 1024
            ),
        )(owners, offsets, points, residual)
        return residual - change_residual, coeffs + change_coeffs

    split = P(None, ("group", "dev"))
    return jax.shard_map(
        body,
        mesh=mesh,
        in_specs=(split, split, split, P(), P()),
        out_specs=(split, split),
        check_vma=False,
    )
```

```python
import functools

import jax
import jax.numpy as jnp
from jax import lax
from jax.experimental import pallas as pl
from jax.experimental.pallas import tpu as pltpu
from jax.sharding import PartitionSpec as P

BLOCK = 256
LANES = 128
SUB = 8

ridge = 2.0
step_norm = 1.5

MESH = pl.DeviceIdType.MESH
F32 = jnp.float32


def exact_dot(a, b, dims):
    return lax.dot_general(
        a, b, (dims, ((), ())), precision=lax.Precision.HIGHEST, preferred_element_type=F32
    )


NN = ((1,), (0,))
NT = ((1,), (1,))


def low_dot(a, b):
    return jnp.dot(a.astype(jnp.bfloat16), b.astype(jnp.bfloat16), preferred_element_type=F32)


def split_dot(a, b, dims=NN):
    ah, bh = a.astype(jnp.bfloat16), b.astype(jnp.bfloat16)
    al = (a - ah.astype(F32)).astype(jnp.bfloat16)
    bl = (b - bh.astype(F32)).astype(jnp.bfloat16)
    dot = lambda u, v: lax.dot_general(u, v, (dims, ((), ())), preferred_element_type=F32)
    return dot(ah, bh) + (dot(ah, bl) + dot(al, bh))


def split_three(x):
    high = x.astype(jnp.bfloat16)
    rest = x - high.astype(F32)
    mid = rest.astype(jnp.bfloat16)
    return high, mid, (rest - mid.astype(F32)).astype(jnp.bfloat16)


def line_width(n_dev):
    width = 1
    while n_dev % (2 * width) == 0 and 4 * width * width <= n_dev:
        width *= 2
    return width


class Layout:
    def __init__(self, n_group, n_dev):
        self.n_dev = n_dev
        self.width = line_width(n_dev)
        self.plane = n_group * self.width
        self.line = n_dev // self.width
        self.cores = 2 if n_group % 2 == 0 else 1
        self.chips = self.plane // self.cores

    def share(self, tiles):
        return -(-tiles // self.plane)


class Sum:
    def __init__(self, layout, at, share, refs):
        self.layout, self.share = layout, share
        self.group, self.dev = at
        self.terms, self.landed, self.held, self.crossed, self.total, self.sems = refs
        self.place = self.group * layout.width + lax.rem(self.dev, layout.width)
        self.plane = self.dev // layout.width
        self.started = []

    def peer_in_plane(self, k):
        to = lax.rem(self.place + k, self.layout.plane)
        width = self.layout.width
        return to, (to // width, self.plane * width + lax.rem(to, width))

    def peer_in_line(self, k):
        to = lax.rem(self.plane + k, self.layout.line)
        width = self.layout.width
        return self.group, to * width + lax.rem(self.dev, width)

    def piece(self, index):
        return pl.ds(index * self.share, self.share)

    def send(self, src, dst, sem, to):
        copy = pltpu.make_async_remote_copy(
            src_ref=src,
            dst_ref=dst,
            send_sem=self.sems.at[0, sem],
            recv_sem=self.sems.at[1, sem],
            device_id=to,
            device_id_type=MESH,
        )
        copy.start()
        self.waiting.append(copy)

    def arrive(self):
        for copy in self.waiting:
            copy.wait_recv()
        self.started += self.waiting

    def scatter(self):
        self.waiting = []
        for k in range(1, self.layout.plane):
            to, device = self.peer_in_plane(k)
            self.send(self.terms.at[self.piece(to)], self.landed.at[self.piece(k - 1)], k - 1, device)

    def cross(self):
        self.arrive()
        total = self.terms[self.piece(self.place)]
        for k in range(self.layout.plane - 1):
            total = total + self.landed[self.piece(k)]
        self.held[...] = total
        self.waiting = []
        first = self.layout.plane - 1
        for k in range(1, self.layout.line):
            self.send(self.held, self.crossed.at[self.piece(k - 1)], first + k - 1, self.peer_in_line(k))

    def gather(self):
        self.arrive()
        total = self.held[...]
        for k in range(self.layout.line - 1):
            total = total + self.crossed[self.piece(k)]
        mine = self.total.at[self.piece(self.place)]
        mine[...] = total
        self.waiting = []
        first = self.layout.plane + self.layout.line - 2
        for k in range(1, self.layout.plane):
            self.send(mine, mine, first + k - 1, self.peer_in_plane(k)[1])

    def relay(self):
        pass

    def forward(self):
        pass

    def finish(self):
        self.arrive()

    def settle(self):
        for copy in self.started:
            copy.wait_send()


class PairedSum(Sum):
    def __init__(self, *args):
        super().__init__(*args)
        layout = self.layout
        self.core = lax.rem(self.group, layout.cores)
        self.chip = (self.group // layout.cores) * layout.width + lax.rem(self.dev, layout.width)
        self.place = self.core * layout.chips + self.chip

    def sibling(self):
        return self.group + 1 - 2 * self.core, self.dev

    def other_chip(self, k):
        layout = self.layout
        to = lax.rem(self.chip + k, layout.chips)
        group = (to // layout.width) * layout.cores + self.core
        return to, (group, self.plane * layout.width + lax.rem(to, layout.width))

    def scatter(self):
        layout = self.layout
        self.waiting = []
        for k in range(1, layout.chips + 1):
            to = (1 - self.core) * layout.chips + lax.rem(self.chip + k, layout.chips)
            self.send(self.terms.at[self.piece(to)], self.landed.at[self.piece(k - 1)], k - 1, self.sibling())

    def relay(self):
        layout = self.layout
        pairs, self.waiting = self.waiting, []
        for k in range(1, layout.chips + 1):
            pairs[k - 1].wait_recv()
            to, device = self.other_chip(k)
            mine = self.piece(self.core * layout.chips + to)
            self.terms[mine] = self.terms[mine] + self.landed[self.piece(k - 1)]
            if k < layout.chips:
                slot = layout.chips + k - 1
                self.send(self.terms.at[mine], self.landed.at[self.piece(slot)], slot, device)
        self.started += pairs

    def cross(self):
        layout = self.layout
        self.arrive()
        total = self.terms[self.piece(self.place)]
        for k in range(1, layout.chips):
            total = total + self.landed[self.piece(layout.chips + k - 1)]
        self.held[...] = total
        self.waiting = []
        first = layout.plane - 1
        for k in range(1, layout.line):
            self.send(self.held, self.crossed.at[self.piece(k - 1)], first + k - 1, self.peer_in_line(k))

    def gather(self):
        layout = self.layout
        self.arrive()
        total = self.held[...]
        for k in range(layout.line - 1):
            total = total + self.crossed[self.piece(k)]
        mine = self.total.at[self.piece(self.place)]
        mine[...] = total
        self.waiting = []
        first = layout.plane + layout.line - 2
        for k in range(1, layout.chips):
            self.send(mine, mine, first + k - 1, self.other_chip(k)[1])
        chips, self.waiting = self.waiting, []
        self.send(mine, mine, first + layout.chips - 1, self.sibling())
        self.chip_copies = chips

    def forward(self):
        layout = self.layout
        first = layout.plane + layout.line - 2 + layout.chips - 1
        for k in range(1, layout.chips):
            self.chip_copies[k - 1].wait_recv()
            source = lax.rem(self.chip + layout.chips - k, layout.chips)
            where = self.total.at[self.piece(self.core * layout.chips + source)]
            self.send(where, where, first + k, self.sibling())
        self.started += self.chip_copies


def sum_scratch(layout, share):
    tile = (SUB, LANES)
    copies = 2 * layout.plane + layout.line - 1
    return [
        pltpu.VMEM((layout.plane * share,) + tile, F32),
        pltpu.VMEM((max(layout.plane - 1, 1) * share,) + tile, F32),
        pltpu.VMEM((share,) + tile, F32),
        pltpu.VMEM((max(layout.line - 1, 1) * share,) + tile, F32),
        pltpu.VMEM((layout.plane * share,) + tile, F32),
        pltpu.SemaphoreType.DMA((2, copies)),
    ]


def to_tiles(ref, value):
    rows, columns = value.shape
    half = rows // SUB
    for c in range(columns // LANES):
        ref[c * half : (c + 1) * half] = value[:, c * LANES : (c + 1) * LANES].reshape(half, SUB, LANES)
    left = ref.shape[0] - half * (columns // LANES)
    if left:
        ref[ref.shape[0] - left :] = jnp.zeros((left, SUB, LANES), F32)


def from_tiles(ref, rows, columns):
    half = rows // SUB
    return jnp.concatenate(
        [ref[c * half : (c + 1) * half].reshape(rows, LANES) for c in range(columns // LANES)], axis=1
    )


def kernel(layout, n_group, owners_in, offsets_in, points_in, residual_in, change, *scratch):
    owners, offsets, points, residual, padded, flipped, tiles, loads = scratch[:8]
    sums = [scratch[8 + 6 * i : 14 + 6 * i] for i in range(4)]
    group, dev = lax.axis_index("group"), lax.axis_index("dev")
    me = group * layout.n_dev + dev
    features, here_points = points.shape
    classes = residual.shape[0]
    rows = padded.shape[0]

    copies = [
        pltpu.make_async_copy(src, dst, loads.at[i])
        for i, (src, dst) in enumerate(
            [(points_in, points), (owners_in, owners), (offsets_in, offsets), (residual_in, residual)]
        )
    ]
    for copy in copies:
        copy.start()

    blocks_share = sums[0][2].shape[0]
    grads_share = sums[2][2].shape[0]
    BlockSum = PairedSum if layout.cores == 2 else Sum
    spread = [BlockSum(layout, (group, dev), blocks_share, sums[i]) for i in range(2)]
    grads = [Sum(layout, (group, dev), grads_share, sums[2 + i]) for i in range(2)]

    barrier = pltpu.get_barrier_semaphore()
    peers = [grads[0].peer_in_plane(k)[1] for k in range(1, layout.plane)]
    peers += [grads[0].peer_in_line(k) for k in range(1, layout.line)]
    for peer in peers:
        pl.semaphore_signal(barrier, inc=1, device_id=peer, device_id_type=MESH)

    def picker(step):
        first = jnp.where(owners[step] == me, offsets[step], 4 * here_points)
        row = lax.broadcasted_iota(jnp.int32, (BLOCK, here_points), 0)
        col = lax.broadcasted_iota(jnp.int32, (BLOCK, here_points), 1)
        return jnp.where(col == row + first, 1.0, 0.0).astype(jnp.bfloat16)

    def pick(step, pieces):
        chosen = picker(step)
        dot = lambda a: lax.dot_general(a, chosen, (NT, ((), ())), preferred_element_type=F32)
        high, mid, low = pieces
        to_tiles(spread[step].terms, (dot(high) + dot(mid)) + dot(low))

    for copy in copies[:3]:
        copy.wait()
    pieces = split_three(points[...])
    pick(0, pieces)
    pl.semaphore_wait(barrier, len(peers))
    spread[0].scatter()
    pick(1, pieces)
    spread[0].relay()
    spread[1].scatter()

    cols = points[...].T
    flipped[...] = cols
    cols_norm = jnp.sum(cols * cols, axis=1, keepdims=True)
    for copy in copies[3:]:
        copy.wait()
    padded[...] = jnp.zeros_like(padded)
    padded[:classes] = residual[...]

    spread[0].cross()
    spread[1].relay()
    spread[0].gather()
    spread[1].cross()
    spread[0].forward()
    spread[0].finish()

    eye = (
        lax.broadcasted_iota(jnp.int32, (BLOCK, BLOCK), 0)
        == lax.broadcasted_iota(jnp.int32, (BLOCK, BLOCK), 1)
    ).astype(F32)

    def kernel_tile(left, left_norm, right):
        cross = exact_dot(left, right, NN)
        right_norm = jnp.sum(right * right, axis=0, keepdims=True)
        return jnp.exp(-(left_norm + right_norm - 2.0 * cross) / features)

    def block(step):
        return from_tiles(spread[step].total, features, BLOCK)

    def make_tile(step):
        tiles[step] = kernel_tile(flipped[...], cols_norm, block(step))

    class Inverse:
        def __init__(self, step):
            b = block(step)
            bt = b.T
            gram = kernel_tile(bt, jnp.sum(bt * bt, axis=1, keepdims=True), b) + ridge * eye
            top = jnp.max(jnp.sum(gram, axis=1, keepdims=True), axis=0, keepdims=True)
            centre = 2.0 / (ridge + top)
            err = (top - ridge) / (top + ridge)
            gain = 2.0 / (2.0 - err * err)
            self.gram = gram
            self.value = (gain * centre) * (2.0 * eye - centre * gram)
            self.err = err * err / (2.0 - err * err)

        def gain(self):
            err = self.err
            self.err = err * err / (2.0 - err * err)
            return 2.0 / (2.0 - err * err)

        def rough(self):
            near = self.value.astype(jnp.bfloat16)
            rest = eye - low_dot(self.gram, near)
            self.value = self.gain() * (near.astype(F32) + low_dot(near, rest))

        def fine(self):
            rest = eye - split_dot(self.gram, self.value)
            self.value = self.gain() * (self.value + low_dot(self.value, rest))

        def polish(self):
            rest = eye - exact_dot(self.gram, self.value, NN)
            self.value = self.value + low_dot(self.value, rest)

    def sum_grad(step):
        to_tiles(grads[step].terms, exact_dot(padded[...], tiles[step], NN))
        grads[step].scatter()

    def make_delta(step, inverse):
        grad = from_tiles(grads[step].total, rows, BLOCK)
        square = jnp.sum(jnp.sum(grad * grad, axis=1, keepdims=True), axis=0, keepdims=True)
        scale = step_norm / jnp.sqrt(square / (classes * BLOCK) + 1e-06)
        return scale * exact_dot(grad, inverse, NN)

    def credit(step, delta):
        chosen = picker(step)
        high, mid, low = split_three(delta)
        dot = lambda a: jnp.dot(a, chosen, preferred_element_type=F32)
        return ((dot(high) + dot(mid)) + dot(low))[:classes]

    make_tile(0)
    sum_grad(0)
    inverse = Inverse(0)
    inverse.rough()
    grads[0].cross()
    spread[1].gather()
    inverse.rough()
    inverse.rough()
    inverse.fine()
    grads[0].gather()
    spread[1].forward()
    inverse.fine()
    inverse.polish()
    spread[1].finish()
    make_tile(1)
    grads[0].finish()
    delta = make_delta(0, inverse.value)
    step = split_dot(delta, tiles[0], NT)
    padded[...] = padded[...] - step
    sum_grad(1)
    change[0] = step[:classes]
    change[1] = credit(0, delta)
    inverse = Inverse(1)
    inverse.rough()
    grads[1].cross()
    inverse.rough()
    inverse.rough()
    inverse.fine()
    grads[1].gather()
    inverse.fine()
    inverse.polish()
    grads[1].finish()
    delta = make_delta(1, inverse.value)
    change[0] = change[0] + split_dot(delta, tiles[1], NT)[:classes]
    change[1] = change[1] + credit(1, delta)
    for each in spread + grads:
        each.settle()


def solution(mesh):
    n_group, n_dev = mesh.shape["group"], mesh.shape["dev"]
    layout = Layout(n_group, n_dev)

    def body(points, residual, coeffs, owners, offsets):
        features, here = points.shape
        classes = residual.shape[0]
        rows = -(-classes // SUB) * SUB
        columns = BLOCK // LANES
        blocks_share = layout.share(features // SUB * columns)
        grads_share = layout.share(rows // SUB * columns)
        vmem = pl.BlockSpec(memory_space=pltpu.VMEM)
        anywhere = pl.BlockSpec(memory_space=pl.ANY)
        change = pl.pallas_call(
            functools.partial(kernel, layout, n_group),
            out_shape=jax.ShapeDtypeStruct((2,) + residual.shape, F32),
            in_specs=[anywhere] * 4,
            out_specs=vmem,
            scratch_shapes=[
                pltpu.SMEM(owners.shape, jnp.int32),
                pltpu.SMEM(offsets.shape, jnp.int32),
                pltpu.VMEM(points.shape, F32),
                pltpu.VMEM(residual.shape, F32),
                pltpu.VMEM((rows, here), F32),
                pltpu.VMEM((here, features), F32),
                pltpu.VMEM((2, here, BLOCK), F32),
                pltpu.SemaphoreType.DMA((4,)),
            ]
            + sum_scratch(layout, blocks_share) * 2
            + sum_scratch(layout, grads_share) * 2,
            compiler_params=pltpu.CompilerParams(
                collective_id=0, has_side_effects=True, vmem_limit_bytes=60 * 1024 * 1024
            ),
        )(owners, offsets, points, residual)
        return residual - change[0], coeffs + change[1]

    split = P(None, ("group", "dev"))
    return jax.shard_map(
        body,
        mesh=mesh,
        in_specs=(split, split, split, P(), P()),
        out_specs=(split, split),
        check_vma=False,
    )
```

```python
import functools

import jax
import jax.numpy as jnp
from jax import lax
from jax.experimental import pallas as pl
from jax.experimental.pallas import tpu as pltpu
from jax.sharding import PartitionSpec as P

BLOCK = 256
LANES = 128
HALVES = BLOCK // LANES
SUB = 8

ridge = 2.0
step_norm = 1.5

MESH = pl.DeviceIdType.MESH
F32 = jnp.float32


def exact_dot(a, b, dims):
    return lax.dot_general(
        a, b, (dims, ((), ())), precision=lax.Precision.HIGHEST, preferred_element_type=F32
    )


NN = ((1,), (0,))
NT = ((1,), (1,))


def low_dot(a, b):
    return jnp.dot(a.astype(jnp.bfloat16), b.astype(jnp.bfloat16), preferred_element_type=F32)


def split_dot(a, b, dims=NN):
    ah, bh = a.astype(jnp.bfloat16), b.astype(jnp.bfloat16)
    al = (a - ah.astype(F32)).astype(jnp.bfloat16)
    bl = (b - bh.astype(F32)).astype(jnp.bfloat16)
    dot = lambda u, v: lax.dot_general(u, v, (dims, ((), ())), preferred_element_type=F32)
    return dot(ah, bh) + (dot(ah, bl) + dot(al, bh))


def split_two(x):
    high = x.astype(jnp.bfloat16)
    return high, (x - high.astype(F32)).astype(jnp.bfloat16)


def joined(parts):
    return parts[0].astype(F32) + parts[1].astype(F32)


def cross_dot(left, right):
    width = right[0].shape[1]
    both = jnp.concatenate(right, axis=1)
    out = jnp.dot(left[0], both, preferred_element_type=F32)
    out = out + jnp.dot(left[1], both, preferred_element_type=F32)
    return out[:, :width] + out[:, width:]


def split_three(x):
    high = x.astype(jnp.bfloat16)
    rest = x - high.astype(F32)
    mid = rest.astype(jnp.bfloat16)
    return high, mid, (rest - mid.astype(F32)).astype(jnp.bfloat16)


def line_width(n_dev):
    width = 1
    while n_dev % (2 * width) == 0 and 4 * width * width <= n_dev:
        width *= 2
    return width


class Layout:
    def __init__(self, n_group, n_dev):
        self.n_dev = n_dev
        self.width = line_width(n_dev)
        self.plane = n_group * self.width
        self.line = n_dev // self.width
        self.cores = 2 if n_group % 2 == 0 else 1
        self.chips = self.plane // self.cores

    def share(self, tiles):
        return -(-tiles // self.plane)


class Sum:
    def __init__(self, layout, at, share, refs):
        self.layout, self.share = layout, share
        self.group, self.dev = at
        self.terms, self.landed, self.held, self.crossed, self.total, self.sems = refs
        self.place = self.group * layout.width + lax.rem(self.dev, layout.width)
        self.plane = self.dev // layout.width
        self.started = []

    def peer_in_plane(self, k):
        to = lax.rem(self.place + k, self.layout.plane)
        width = self.layout.width
        return to, (to // width, self.plane * width + lax.rem(to, width))

    def peer_in_line(self, k):
        to = lax.rem(self.plane + k, self.layout.line)
        width = self.layout.width
        return self.group, to * width + lax.rem(self.dev, width)

    def piece(self, index):
        return pl.ds(index * self.share, self.share)

    def send(self, src, dst, sem, to):
        copy = pltpu.make_async_remote_copy(
            src_ref=src,
            dst_ref=dst,
            send_sem=self.sems.at[0, sem],
            recv_sem=self.sems.at[1, sem],
            device_id=to,
            device_id_type=MESH,
        )
        copy.start()
        self.waiting.append(copy)

    def arrive(self):
        for copy in self.waiting:
            copy.wait_recv()
        self.started += self.waiting

    def scatter(self):
        self.waiting = []
        for k in range(1, self.layout.plane):
            to, device = self.peer_in_plane(k)
            self.send(self.terms.at[self.piece(to)], self.landed.at[self.piece(k - 1)], k - 1, device)

    def cross(self):
        self.arrive()
        total = self.terms[self.piece(self.place)]
        for k in range(self.layout.plane - 1):
            total = total + self.landed[self.piece(k)]
        self.held[...] = total
        self.waiting = []
        first = self.layout.plane - 1
        for k in range(1, self.layout.line):
            self.send(self.held, self.crossed.at[self.piece(k - 1)], first + k - 1, self.peer_in_line(k))

    def gather(self):
        self.arrive()
        total = self.held[...]
        for k in range(self.layout.line - 1):
            total = total + self.crossed[self.piece(k)]
        mine = self.total.at[self.piece(self.place)]
        mine[...] = total
        self.waiting = []
        first = self.layout.plane + self.layout.line - 2
        for k in range(1, self.layout.plane):
            self.send(mine, mine, first + k - 1, self.peer_in_plane(k)[1])

    def relay(self):
        pass

    def forward(self):
        pass

    def finish(self):
        self.arrive()

    def settle(self):
        for copy in self.started:
            copy.wait_send()


class PairedSum(Sum):
    def __init__(self, *args):
        super().__init__(*args)
        layout = self.layout
        self.core = lax.rem(self.group, layout.cores)
        self.chip = (self.group // layout.cores) * layout.width + lax.rem(self.dev, layout.width)
        self.place = self.core * layout.chips + self.chip

    def sibling(self):
        return self.group + 1 - 2 * self.core, self.dev

    def other_chip(self, k):
        layout = self.layout
        to = lax.rem(self.chip + k, layout.chips)
        group = (to // layout.width) * layout.cores + self.core
        return to, (group, self.plane * layout.width + lax.rem(to, layout.width))

    def scatter(self):
        layout = self.layout
        self.waiting = []
        for k in range(1, layout.chips + 1):
            to = (1 - self.core) * layout.chips + lax.rem(self.chip + k, layout.chips)
            self.send(self.terms.at[self.piece(to)], self.landed.at[self.piece(k - 1)], k - 1, self.sibling())

    def relay(self):
        layout = self.layout
        pairs, self.waiting = self.waiting, []
        for k in range(1, layout.chips + 1):
            pairs[k - 1].wait_recv()
            to, device = self.other_chip(k)
            mine = self.piece(self.core * layout.chips + to)
            self.terms[mine] = self.terms[mine] + self.landed[self.piece(k - 1)]
            if k < layout.chips:
                slot = layout.chips + k - 1
                self.send(self.terms.at[mine], self.landed.at[self.piece(slot)], slot, device)
        self.started += pairs

    def cross(self):
        layout = self.layout
        self.arrive()
        total = self.terms[self.piece(self.place)]
        for k in range(1, layout.chips):
            total = total + self.landed[self.piece(layout.chips + k - 1)]
        self.held[...] = total
        self.waiting = []
        first = layout.plane - 1
        for k in range(1, layout.line):
            self.send(self.held, self.crossed.at[self.piece(k - 1)], first + k - 1, self.peer_in_line(k))

    def gather(self):
        layout = self.layout
        self.arrive()
        total = self.held[...]
        for k in range(layout.line - 1):
            total = total + self.crossed[self.piece(k)]
        mine = self.total.at[self.piece(self.place)]
        mine[...] = total
        self.waiting = []
        first = layout.plane + layout.line - 2
        for k in range(1, layout.chips):
            self.send(mine, mine, first + k - 1, self.other_chip(k)[1])
        chips, self.waiting = self.waiting, []
        self.send(mine, mine, first + layout.chips - 1, self.sibling())
        self.chip_copies = chips

    def forward(self):
        layout = self.layout
        first = layout.plane + layout.line - 2 + layout.chips - 1
        for k in range(1, layout.chips):
            self.chip_copies[k - 1].wait_recv()
            source = lax.rem(self.chip + layout.chips - k, layout.chips)
            where = self.total.at[self.piece(self.core * layout.chips + source)]
            self.send(where, where, first + k, self.sibling())
        self.started += self.chip_copies


def sum_scratch(layout, share):
    tile = (SUB, LANES)
    copies = 2 * layout.plane + layout.line - 1
    return [
        pltpu.VMEM((layout.plane * share,) + tile, F32),
        pltpu.VMEM((max(layout.plane - 1, 1) * share,) + tile, F32),
        pltpu.VMEM((share,) + tile, F32),
        pltpu.VMEM((max(layout.line - 1, 1) * share,) + tile, F32),
        pltpu.VMEM((layout.plane * share,) + tile, F32),
        pltpu.SemaphoreType.DMA((2, copies)),
    ]


def to_tiles(ref, value):
    rows, columns = value.shape
    half = rows // SUB
    for c in range(columns // LANES):
        ref[c * half : (c + 1) * half] = value[:, c * LANES : (c + 1) * LANES].reshape(half, SUB, LANES)
    left = ref.shape[0] - half * (columns // LANES)
    if left:
        ref[ref.shape[0] - left :] = jnp.zeros((left, SUB, LANES), F32)


def from_tiles(ref, rows, columns):
    half = rows // SUB
    return jnp.concatenate(
        [ref[c * half : (c + 1) * half].reshape(rows, LANES) for c in range(columns // LANES)], axis=1
    )


def kernel(layout, n_group, owners_in, offsets_in, points_in, residual_in, change, *scratch):
    owners, offsets, points, residual, padded, flipped, tiles, loads = scratch[:8]
    sums = [scratch[8 + 6 * i : 14 + 6 * i] for i in range(2 * HALVES + 2)]
    group, dev = lax.axis_index("group"), lax.axis_index("dev")
    me = group * layout.n_dev + dev
    features, here_points = points.shape
    classes = residual.shape[0]
    rows = padded.shape[0]

    copies = [
        pltpu.make_async_copy(src, dst, loads.at[i])
        for i, (src, dst) in enumerate(
            [(points_in, points), (owners_in, owners), (offsets_in, offsets), (residual_in, residual)]
        )
    ]
    for copy in copies:
        copy.start()

    blocks_share = sums[0][2].shape[0]
    grads_share = sums[-1][2].shape[0]
    BlockSum = PairedSum if layout.cores == 2 else Sum
    at = (group, dev)
    spread = [BlockSum(layout, at, blocks_share, refs) for refs in sums[: 2 * HALVES]]
    grads = [Sum(layout, at, grads_share, refs) for refs in sums[2 * HALVES :]]
    left0, right0, left1, right1 = spread

    barrier = pltpu.get_barrier_semaphore()
    peers = [grads[0].peer_in_plane(k)[1] for k in range(1, layout.plane)]
    peers += [grads[0].peer_in_line(k) for k in range(1, layout.line)]
    for peer in peers:
        pl.semaphore_signal(barrier, inc=1, device_id=peer, device_id_type=MESH)

    def picker(step):
        first = jnp.where(owners[step] == me, offsets[step], 4 * here_points)
        row = lax.broadcasted_iota(jnp.int32, (BLOCK, here_points), 0)
        col = lax.broadcasted_iota(jnp.int32, (BLOCK, here_points), 1)
        return jnp.where(col == row + first, 1.0, 0.0).astype(jnp.bfloat16)

    def pick(index):
        chosen = picker(index // HALVES)
        at = index % HALVES * LANES
        chosen = chosen[at : at + LANES]
        dot = lambda a: lax.dot_general(a, chosen, (NT, ((), ())), preferred_element_type=F32)
        high, mid, low = pieces
        to_tiles(spread[index].terms, (dot(high) + dot(mid)) + dot(low))

    for copy in copies[:3]:
        copy.wait()
    pieces = split_three(points[...])
    pick(0)
    pl.semaphore_wait(barrier, len(peers))
    left0.scatter()
    pick(1)
    left0.relay()
    right0.scatter()
    pick(2)
    left0.cross()
    right0.relay()
    left1.scatter()
    pick(3)

    cols = split_two(points[...].T)
    flipped[0], flipped[1] = cols
    cols = joined(cols)
    cols_norm = jnp.sum(cols * cols, axis=1, keepdims=True)
    for copy in copies[3:]:
        copy.wait()
    padded[...] = jnp.zeros_like(padded)
    padded[:classes] = residual[...]

    left0.gather()
    right0.cross()
    left1.relay()
    right1.scatter()
    left0.forward()
    right0.gather()
    left1.cross()
    right1.relay()

    eye = (
        lax.broadcasted_iota(jnp.int32, (BLOCK, BLOCK), 0)
        == lax.broadcasted_iota(jnp.int32, (BLOCK, BLOCK), 1)
    ).astype(F32)

    def kernel_tile(left, left_norm, right):
        right = split_two(right)
        whole = joined(right)
        right_norm = jnp.sum(whole * whole, axis=0, keepdims=True)
        return jnp.exp(-(left_norm + right_norm - 2.0 * cross_dot(left, right)) / features)

    def half_block(index):
        return from_tiles(spread[index].total, features, LANES)

    def half_tile(index):
        spread[index].finish()
        at = index % HALVES * LANES
        tiles[index // HALVES, :, at : at + LANES] = kernel_tile(
            (flipped[0], flipped[1]), cols_norm, half_block(index)
        )

    class Inverse:
        def __init__(self, step):
            halves = [half_block(HALVES * step + h) for h in range(HALVES)]
            b = jnp.concatenate(halves, axis=1)
            rows = split_two(b.T)
            whole = joined(rows)
            gram = kernel_tile(rows, jnp.sum(whole * whole, axis=1, keepdims=True), b) + ridge * eye
            top = jnp.max(jnp.sum(gram, axis=1, keepdims=True), axis=0, keepdims=True)
            centre = 2.0 / (ridge + top)
            err = (top - ridge) / (top + ridge)
            gain = 2.0 / (2.0 - err * err)
            self.gram = gram
            self.value = (gain * centre) * (2.0 * eye - centre * gram)
            self.err = err * err / (2.0 - err * err)

        def gain(self):
            err = self.err
            self.err = err * err / (2.0 - err * err)
            return 2.0 / (2.0 - err * err)

        def rough(self):
            near = self.value.astype(jnp.bfloat16)
            rest = eye - low_dot(self.gram, near)
            self.value = self.gain() * (near.astype(F32) + low_dot(near, rest))

        def fine(self):
            rest = eye - split_dot(self.gram, self.value)
            self.value = self.gain() * (self.value + low_dot(self.value, rest))

        def polish(self):
            rest = eye - exact_dot(self.gram, self.value, NN)
            self.value = self.value + low_dot(self.value, rest)

    def sum_grad(step):
        to_tiles(grads[step].terms, exact_dot(padded[...], tiles[step], NN))
        grads[step].scatter()

    def make_delta(step, inverse):
        grad = from_tiles(grads[step].total, rows, BLOCK)
        square = jnp.sum(jnp.sum(grad * grad, axis=1, keepdims=True), axis=0, keepdims=True)
        scale = step_norm / jnp.sqrt(square / (classes * BLOCK) + 1e-06)
        return scale * exact_dot(grad, inverse, NN)

    def credit(step, delta):
        chosen = picker(step)
        high, mid, low = split_three(delta)
        dot = lambda a: jnp.dot(a, chosen, preferred_element_type=F32)
        return ((dot(high) + dot(mid)) + dot(low))[:classes]

    half_tile(0)
    right0.forward()
    right1.cross()
    half_tile(1)
    sum_grad(0)
    inverse = Inverse(0)
    inverse.rough()
    grads[0].cross()
    left1.gather()
    right1.gather()
    inverse.rough()
    inverse.rough()
    inverse.fine()
    left1.forward()
    right1.forward()
    grads[0].gather()
    inverse.fine()
    inverse.polish()
    half_tile(2)
    half_tile(3)
    grads[0].finish()
    delta = make_delta(0, inverse.value)
    step = split_dot(delta, tiles[0], NT)
    padded[...] = padded[...] - step
    sum_grad(1)
    change[0] = step[:classes]
    change[1] = credit(0, delta)
    inverse = Inverse(1)
    inverse.rough()
    grads[1].cross()
    inverse.rough()
    inverse.rough()
    inverse.fine()
    grads[1].gather()
    inverse.fine()
    inverse.polish()
    grads[1].finish()
    delta = make_delta(1, inverse.value)
    change[0] = change[0] + split_dot(delta, tiles[1], NT)[:classes]
    change[1] = change[1] + credit(1, delta)
    for each in spread + grads:
        each.settle()


def solution(mesh):
    n_group, n_dev = mesh.shape["group"], mesh.shape["dev"]
    layout = Layout(n_group, n_dev)

    def body(points, residual, coeffs, owners, offsets):
        features, here = points.shape
        classes = residual.shape[0]
        rows = -(-classes // SUB) * SUB
        blocks_share = layout.share(features // SUB)
        grads_share = layout.share(rows // SUB * HALVES)
        vmem = pl.BlockSpec(memory_space=pltpu.VMEM)
        anywhere = pl.BlockSpec(memory_space=pl.ANY)
        change = pl.pallas_call(
            functools.partial(kernel, layout, n_group),
            out_shape=jax.ShapeDtypeStruct((2,) + residual.shape, F32),
            in_specs=[anywhere] * 4,
            out_specs=vmem,
            scratch_shapes=[
                pltpu.SMEM(owners.shape, jnp.int32),
                pltpu.SMEM(offsets.shape, jnp.int32),
                pltpu.VMEM(points.shape, F32),
                pltpu.VMEM(residual.shape, F32),
                pltpu.VMEM((rows, here), F32),
                pltpu.VMEM((2, here, features), jnp.bfloat16),
                pltpu.VMEM((2, here, BLOCK), F32),
                pltpu.SemaphoreType.DMA((4,)),
            ]
            + sum_scratch(layout, blocks_share) * (2 * HALVES)
            + sum_scratch(layout, grads_share) * 2,
            compiler_params=pltpu.CompilerParams(
                collective_id=0, has_side_effects=True, vmem_limit_bytes=60 * 1024 * 1024
            ),
        )(owners, offsets, points, residual)
        return residual - change[0], coeffs + change[1]

    split = P(None, ("group", "dev"))
    return jax.shard_map(
        body,
        mesh=mesh,
        in_specs=(split, split, split, P(), P()),
        out_specs=(split, split),
        check_vma=False,
    )
```

```python
import functools

import jax
import jax.numpy as jnp
from jax import lax
from jax.experimental import pallas as pl
from jax.experimental.pallas import tpu as pltpu
from jax.sharding import PartitionSpec as P

BLOCK = 256
LANES = 128
HALVES = BLOCK // LANES
SUB = 8

ridge = 2.0
step_norm = 1.5

MESH = pl.DeviceIdType.MESH
F32 = jnp.float32


def exact_dot(a, b, dims):
    return lax.dot_general(
        a, b, (dims, ((), ())), precision=lax.Precision.HIGHEST, preferred_element_type=F32
    )


NN = ((1,), (0,))
NT = ((1,), (1,))


def low_dot(a, b):
    return jnp.dot(a.astype(jnp.bfloat16), b.astype(jnp.bfloat16), preferred_element_type=F32)


def split_dot(a, b, dims=NN):
    ah, bh = a.astype(jnp.bfloat16), b.astype(jnp.bfloat16)
    al = (a - ah.astype(F32)).astype(jnp.bfloat16)
    bl = (b - bh.astype(F32)).astype(jnp.bfloat16)
    dot = lambda u, v: lax.dot_general(u, v, (dims, ((), ())), preferred_element_type=F32)
    return dot(ah, bh) + (dot(ah, bl) + dot(al, bh))


def split_two(x):
    high = x.astype(jnp.bfloat16)
    return high, (x - high.astype(F32)).astype(jnp.bfloat16)


def joined(parts):
    return parts[0].astype(F32) + parts[1].astype(F32)


def cross_dot(left, right):
    width = right[0].shape[1]
    both = jnp.concatenate(right, axis=1)
    out = jnp.dot(left[0], both, preferred_element_type=F32)
    out = out + jnp.dot(left[1], both, preferred_element_type=F32)
    return out[:, :width] + out[:, width:]


def split_three(x):
    high = x.astype(jnp.bfloat16)
    rest = x - high.astype(F32)
    mid = rest.astype(jnp.bfloat16)
    return high, mid, (rest - mid.astype(F32)).astype(jnp.bfloat16)


def line_width(n_dev):
    width = 1
    while n_dev % (2 * width) == 0 and 4 * width * width <= n_dev:
        width *= 2
    return width


class Layout:
    def __init__(self, n_group, n_dev):
        self.n_dev = n_dev
        self.width = line_width(n_dev)
        self.plane = n_group * self.width
        self.line = n_dev // self.width
        self.cores = 2 if n_group % 2 == 0 else 1
        self.chips = self.plane // self.cores

    def share(self, tiles):
        return -(-tiles // self.plane)


class Sum:
    def __init__(self, layout, at, share, refs):
        self.layout, self.share = layout, share
        self.group, self.dev = at
        self.terms, self.landed, self.held, self.crossed, self.total, self.sems = refs
        self.place = self.group * layout.width + lax.rem(self.dev, layout.width)
        self.plane = self.dev // layout.width
        self.sent = {}

    def peer_in_plane(self, k):
        to = lax.rem(self.place + k, self.layout.plane)
        width = self.layout.width
        return to, (to // width, self.plane * width + lax.rem(to, width))

    def peer_in_line(self, k):
        to = lax.rem(self.plane + k, self.layout.line)
        width = self.layout.width
        return self.group, to * width + lax.rem(self.dev, width)

    def piece(self, index):
        return pl.ds(index * self.share, self.share)

    def send(self, src, dst, to, out_sem, in_sem):
        pltpu.make_async_remote_copy(
            src_ref=src,
            dst_ref=dst,
            send_sem=self.sems.at[0, out_sem],
            recv_sem=self.sems.at[1, in_sem],
            device_id=to,
            device_id_type=MESH,
        ).start()
        self.sent[out_sem] = self.sent.get(out_sem, 0) + 1

    def wait(self, way, sem, count):
        if count:
            like = self.terms.at[pl.ds(0, count * self.share)]
            pltpu.make_async_copy(like, like, self.sems.at[way, sem]).wait()

    def scatter(self):
        for k in range(1, self.layout.plane):
            to, device = self.peer_in_plane(k)
            self.send(self.terms.at[self.piece(to)], self.landed.at[self.piece(k - 1)], device, 0, 0)

    def cross(self):
        self.wait(1, 0, self.layout.plane - 1)
        total = self.terms[self.piece(self.place)]
        for k in range(self.layout.plane - 1):
            total = total + self.landed[self.piece(k)]
        self.held[...] = total
        for k in range(1, self.layout.line):
            self.send(self.held, self.crossed.at[self.piece(k - 1)], self.peer_in_line(k), 1, 1)

    def gather(self):
        self.wait(1, 1, self.layout.line - 1)
        mine = self.total.at[self.piece(self.place)]
        total = self.held[...]
        for k in range(self.layout.line - 1):
            total = total + self.crossed[self.piece(k)]
        mine[...] = total
        for k in range(1, self.layout.plane):
            self.send(mine, mine, self.peer_in_plane(k)[1], 2, 2)

    def relay(self):
        pass

    def forward(self):
        pass

    def finish(self):
        self.wait(1, 2, self.layout.plane - 1)

    def settle(self):
        for sem, count in sorted(self.sent.items()):
            self.wait(0, sem, count)


class PairedSum(Sum):
    def __init__(self, *args):
        super().__init__(*args)
        layout = self.layout
        self.core = lax.rem(self.group, layout.cores)
        self.chip = (self.group // layout.cores) * layout.width + lax.rem(self.dev, layout.width)
        self.place = self.core * layout.chips + self.chip

    def sibling(self):
        return self.group + 1 - 2 * self.core, self.dev

    def other_chip(self, k):
        layout = self.layout
        to = lax.rem(self.chip + k, layout.chips)
        group = (to // layout.width) * layout.cores + self.core
        return to, (group, self.plane * layout.width + lax.rem(to, layout.width))

    def scatter(self):
        chips = self.layout.chips
        for k in range(1, chips + 1):
            to = (1 - self.core) * chips + lax.rem(self.chip + k, chips)
            src, dst = self.terms.at[self.piece(to)], self.landed.at[self.piece(k - 1)]
            self.send(src, dst, self.sibling(), 0, k - 1)

    def relay(self):
        chips = self.layout.chips
        for k in range(1, chips + 1):
            self.wait(1, k - 1, 1)
            to, device = self.other_chip(k)
            mine = self.piece(self.core * chips + to)
            self.terms[mine] = self.terms[mine] + self.landed[self.piece(k - 1)]
            if k < chips:
                self.send(self.terms.at[mine], self.landed.at[self.piece(chips + k - 1)], device, 1, chips)

    def cross(self):
        layout, chips = self.layout, self.layout.chips
        self.wait(1, chips, chips - 1)
        total = self.terms[self.piece(self.place)]
        for k in range(1, chips):
            total = total + self.landed[self.piece(chips + k - 1)]
        self.held[...] = total
        for k in range(1, layout.line):
            self.send(self.held, self.crossed.at[self.piece(k - 1)], self.peer_in_line(k), 2, chips + 1)

    def gather(self):
        layout, chips = self.layout, self.layout.chips
        self.wait(1, chips + 1, layout.line - 1)
        total = self.held[...]
        for k in range(layout.line - 1):
            total = total + self.crossed[self.piece(k)]
        mine = self.total.at[self.piece(self.place)]
        mine[...] = total
        for k in range(1, chips):
            self.send(mine, mine, self.other_chip(k)[1], 3, chips + 1 + k)
        self.send(mine, mine, self.sibling(), 4, 2 * chips + 1)

    def forward(self):
        chips = self.layout.chips
        for k in range(1, chips):
            self.wait(1, chips + 1 + k, 1)
            source = lax.rem(self.chip + chips - k, chips)
            where = self.total.at[self.piece(self.core * chips + source)]
            self.send(where, where, self.sibling(), 4, 2 * chips + 1)

    def finish(self):
        self.wait(1, 2 * self.layout.chips + 1, self.layout.chips)


def sum_scratch(layout, share):
    tile = (SUB, LANES)
    sems = 2 * layout.chips + 5
    return [
        pltpu.VMEM((layout.plane * share,) + tile, F32),
        pltpu.VMEM((max(layout.plane - 1, 1) * share,) + tile, F32),
        pltpu.VMEM((share,) + tile, F32),
        pltpu.VMEM((max(layout.line - 1, 1) * share,) + tile, F32),
        pltpu.VMEM((layout.plane * share,) + tile, F32),
        pltpu.SemaphoreType.DMA((2, sems)),
    ]


def to_tiles(ref, value):
    rows, columns = value.shape
    half = rows // SUB
    for c in range(columns // LANES):
        ref[c * half : (c + 1) * half] = value[:, c * LANES : (c + 1) * LANES].reshape(half, SUB, LANES)
    left = ref.shape[0] - half * (columns // LANES)
    if left:
        ref[ref.shape[0] - left :] = jnp.zeros((left, SUB, LANES), F32)


def from_tiles(ref, rows, columns):
    half = rows // SUB
    return jnp.concatenate(
        [ref[c * half : (c + 1) * half].reshape(rows, LANES) for c in range(columns // LANES)], axis=1
    )


def kernel(layout, n_group, owners_in, offsets_in, points_in, residual_in, change, *scratch):
    owners, offsets, points, residual, padded, flipped, tiles, loads = scratch[:8]
    sums = [scratch[8 + 6 * i : 14 + 6 * i] for i in range(2 * HALVES + 2)]
    group, dev = lax.axis_index("group"), lax.axis_index("dev")
    me = group * layout.n_dev + dev
    features, here_points = points.shape
    classes = residual.shape[0]
    rows = padded.shape[0]

    copies = [
        pltpu.make_async_copy(src, dst, loads.at[i])
        for i, (src, dst) in enumerate(
            [(points_in, points), (owners_in, owners), (offsets_in, offsets), (residual_in, residual)]
        )
    ]
    for copy in copies:
        copy.start()

    blocks_share = sums[0][2].shape[0]
    grads_share = sums[-1][2].shape[0]
    BlockSum = PairedSum if layout.cores == 2 else Sum
    at = (group, dev)
    spread = [BlockSum(layout, at, blocks_share, refs) for refs in sums[: 2 * HALVES]]
    grads = [Sum(layout, at, grads_share, refs) for refs in sums[2 * HALVES :]]
    left0, right0, left1, right1 = spread

    barrier = pltpu.get_barrier_semaphore()
    peers = [grads[0].peer_in_plane(k)[1] for k in range(1, layout.plane)]
    peers += [grads[0].peer_in_line(k) for k in range(1, layout.line)]
    for peer in peers:
        pl.semaphore_signal(barrier, inc=1, device_id=peer, device_id_type=MESH)

    def picker(step):
        first = jnp.where(owners[step] == me, offsets[step], 4 * here_points)
        row = lax.broadcasted_iota(jnp.int32, (BLOCK, here_points), 0)
        col = lax.broadcasted_iota(jnp.int32, (BLOCK, here_points), 1)
        return jnp.where(col == row + first, 1.0, 0.0).astype(jnp.bfloat16)

    def pick(index):
        chosen = picker(index // HALVES)
        at = index % HALVES * LANES
        chosen = chosen[at : at + LANES]
        dot = lambda a: lax.dot_general(a, chosen, (NT, ((), ())), preferred_element_type=F32)
        high, mid, low = pieces
        to_tiles(spread[index].terms, (dot(high) + dot(mid)) + dot(low))

    for copy in copies[:3]:
        copy.wait()
    pieces = split_three(points[...])
    pick(0)
    pl.semaphore_wait(barrier, len(peers))
    left0.scatter()
    pick(1)
    left0.relay()
    right0.scatter()
    cols = split_two(points[...].T)
    flipped[0], flipped[1] = cols
    right0.relay()
    left0.cross()
    cols = joined(cols)
    cols_norm = jnp.sum(cols * cols, axis=1, keepdims=True)
    right0.cross()
    pick(2)
    left1.scatter()
    for copy in copies[3:]:
        copy.wait()
    padded[...] = jnp.zeros_like(padded)
    padded[:classes] = residual[...]
    left0.gather()
    left1.relay()
    pick(3)
    right1.scatter()
    right0.gather()
    left1.cross()
    left0.forward()
    right1.relay()

    eye = (
        lax.broadcasted_iota(jnp.int32, (BLOCK, BLOCK), 0)
        == lax.broadcasted_iota(jnp.int32, (BLOCK, BLOCK), 1)
    ).astype(F32)

    def kernel_tile(left, left_norm, right):
        right = split_two(right)
        whole = joined(right)
        right_norm = jnp.sum(whole * whole, axis=0, keepdims=True)
        return jnp.exp(-(left_norm + right_norm - 2.0 * cross_dot(left, right)) / features)

    def half_block(index):
        return from_tiles(spread[index].total, features, LANES)

    def half_tile(index):
        spread[index].finish()
        at = index % HALVES * LANES
        tiles[index // HALVES, :, at : at + LANES] = kernel_tile(
            (flipped[0], flipped[1]), cols_norm, half_block(index)
        )

    class Inverse:
        def __init__(self, step):
            halves = [half_block(HALVES * step + h) for h in range(HALVES)]
            b = jnp.concatenate(halves, axis=1)
            rows = split_two(b.T)
            whole = joined(rows)
            gram = kernel_tile(rows, jnp.sum(whole * whole, axis=1, keepdims=True), b) + ridge * eye
            top = jnp.max(jnp.sum(gram, axis=1, keepdims=True), axis=0, keepdims=True)
            centre = 2.0 / (ridge + top)
            err = (top - ridge) / (top + ridge)
            gain = 2.0 / (2.0 - err * err)
            self.gram = gram
            self.value = (gain * centre) * (2.0 * eye - centre * gram)
            self.err = err * err / (2.0 - err * err)

        def gain(self):
            err = self.err
            self.err = err * err / (2.0 - err * err)
            return 2.0 / (2.0 - err * err)

        def rough(self):
            near = self.value.astype(jnp.bfloat16)
            rest = eye - low_dot(self.gram, near)
            self.value = self.gain() * (near.astype(F32) + low_dot(near, rest))

        def fine(self):
            rest = eye - split_dot(self.gram, self.value)
            self.value = self.gain() * (self.value + low_dot(self.value, rest))

        def polish(self):
            rest = eye - exact_dot(self.gram, self.value, NN)
            self.value = self.value + low_dot(self.value, rest)

    def sum_grad(step):
        to_tiles(grads[step].terms, exact_dot(padded[...], tiles[step], NN))
        grads[step].scatter()

    def make_delta(step, inverse):
        grad = from_tiles(grads[step].total, rows, BLOCK)
        square = jnp.sum(jnp.sum(grad * grad, axis=1, keepdims=True), axis=0, keepdims=True)
        scale = step_norm / jnp.sqrt(square / (classes * BLOCK) + 1e-06)
        return scale * exact_dot(grad, inverse, NN)

    def credit(step, delta):
        chosen = picker(step)
        high, mid, low = split_three(delta)
        dot = lambda a: jnp.dot(a, chosen, preferred_element_type=F32)
        return ((dot(high) + dot(mid)) + dot(low))[:classes]

    half_tile(0)
    right0.forward()
    right1.cross()
    half_tile(1)
    sum_grad(0)
    inverse = Inverse(0)
    inverse.rough()
    grads[0].cross()
    left1.gather()
    right1.gather()
    inverse.rough()
    inverse.rough()
    inverse.fine()
    left1.forward()
    right1.forward()
    grads[0].gather()
    inverse.fine()
    inverse.polish()
    half_tile(2)
    half_tile(3)
    grads[0].finish()
    delta = make_delta(0, inverse.value)
    step = split_dot(delta, tiles[0], NT)
    padded[...] = padded[...] - step
    sum_grad(1)
    change[0] = step[:classes]
    change[1] = credit(0, delta)
    inverse = Inverse(1)
    inverse.rough()
    grads[1].cross()
    for each in spread:
        each.settle()
    grads[0].settle()
    inverse.rough()
    inverse.rough()
    inverse.fine()
    grads[1].gather()
    inverse.fine()
    inverse.polish()
    grads[1].finish()
    delta = make_delta(1, inverse.value)
    change[0] = change[0] + split_dot(delta, tiles[1], NT)[:classes]
    change[1] = change[1] + credit(1, delta)
    grads[1].settle()


def solution(mesh):
    n_group, n_dev = mesh.shape["group"], mesh.shape["dev"]
    layout = Layout(n_group, n_dev)

    def body(points, residual, coeffs, owners, offsets):
        features, here = points.shape
        classes = residual.shape[0]
        rows = -(-classes // SUB) * SUB
        blocks_share = layout.share(features // SUB)
        grads_share = layout.share(rows // SUB * HALVES)
        vmem = pl.BlockSpec(memory_space=pltpu.VMEM)
        anywhere = pl.BlockSpec(memory_space=pl.ANY)
        change = pl.pallas_call(
            functools.partial(kernel, layout, n_group),
            out_shape=jax.ShapeDtypeStruct((2,) + residual.shape, F32),
            in_specs=[anywhere] * 4,
            out_specs=vmem,
            scratch_shapes=[
                pltpu.SMEM(owners.shape, jnp.int32),
                pltpu.SMEM(offsets.shape, jnp.int32),
                pltpu.VMEM(points.shape, F32),
                pltpu.VMEM(residual.shape, F32),
                pltpu.VMEM((rows, here), F32),
                pltpu.VMEM((2, here, features), jnp.bfloat16),
                pltpu.VMEM((2, here, BLOCK), F32),
                pltpu.SemaphoreType.DMA((4,)),
            ]
            + sum_scratch(layout, blocks_share) * (2 * HALVES)
            + sum_scratch(layout, grads_share) * 2,
            compiler_params=pltpu.CompilerParams(
                collective_id=0, has_side_effects=True, vmem_limit_bytes=60 * 1024 * 1024
            ),
        )(owners, offsets, points, residual)
        return residual - change[0], coeffs + change[1]

    split = P(None, ("group", "dev"))
    return jax.shard_map(
        body,
        mesh=mesh,
        in_specs=(split, split, split, P(), P()),
        out_specs=(split, split),
        check_vma=False,
    )
```

```python
import functools

import jax
import jax.numpy as jnp
from jax import lax
from jax.experimental import pallas as pl
from jax.experimental.pallas import tpu as pltpu
from jax.sharding import PartitionSpec as P

BLOCK = 256
LANES = 128
HALVES = BLOCK // LANES
SUB = 8

ridge = 2.0
step_norm = 1.5

MESH = pl.DeviceIdType.MESH
F32 = jnp.float32


def exact_dot(a, b, dims):
    return lax.dot_general(
        a, b, (dims, ((), ())), precision=lax.Precision.HIGHEST, preferred_element_type=F32
    )


NN = ((1,), (0,))
NT = ((1,), (1,))


def low_dot(a, b):
    return jnp.dot(a.astype(jnp.bfloat16), b.astype(jnp.bfloat16), preferred_element_type=F32)


def split_dot(a, b, dims=NN):
    ah, bh = a.astype(jnp.bfloat16), b.astype(jnp.bfloat16)
    al = (a - ah.astype(F32)).astype(jnp.bfloat16)
    bl = (b - bh.astype(F32)).astype(jnp.bfloat16)
    dot = lambda u, v: lax.dot_general(u, v, (dims, ((), ())), preferred_element_type=F32)
    return dot(ah, bh) + (dot(ah, bl) + dot(al, bh))


def split_two(x):
    high = x.astype(jnp.bfloat16)
    return high, (x - high.astype(F32)).astype(jnp.bfloat16)


def joined(parts):
    return parts[0].astype(F32) + parts[1].astype(F32)


def cross_dot(left, right):
    width = right[0].shape[1]
    both = jnp.concatenate(right, axis=1)
    out = jnp.dot(left[0], both, preferred_element_type=F32)
    out = out + jnp.dot(left[1], both, preferred_element_type=F32)
    return out[:, :width] + out[:, width:]


def split_three(x):
    high = x.astype(jnp.bfloat16)
    rest = x - high.astype(F32)
    mid = rest.astype(jnp.bfloat16)
    return high, mid, (rest - mid.astype(F32)).astype(jnp.bfloat16)


def line_width(n_dev):
    width = 1
    while n_dev % (2 * width) == 0 and 4 * width * width <= n_dev:
        width *= 2
    return width


class Layout:
    def __init__(self, n_group, n_dev):
        self.n_dev = n_dev
        self.width = line_width(n_dev)
        self.plane = n_group * self.width
        self.line = n_dev // self.width
        self.cores = 2 if n_group % 2 == 0 else 1
        self.chips = self.plane // self.cores

    def share(self, tiles):
        return -(-tiles // self.plane)


class Sum:
    def __init__(self, layout, at, share, refs):
        self.layout, self.share = layout, share
        self.group, self.dev = at
        self.terms, self.landed, self.held, self.crossed, self.total, self.sems = refs
        self.place = self.group * layout.width + lax.rem(self.dev, layout.width)
        self.plane = self.dev // layout.width
        self.sent = {}

    def peer_in_plane(self, k):
        to = lax.rem(self.place + k, self.layout.plane)
        width = self.layout.width
        return to, (to // width, self.plane * width + lax.rem(to, width))

    def peer_in_line(self, k):
        to = lax.rem(self.plane + k, self.layout.line)
        width = self.layout.width
        return self.group, to * width + lax.rem(self.dev, width)

    def piece(self, index):
        return pl.ds(index * self.share, self.share)

    def send(self, src, dst, to, out_sem, in_sem, pieces=1):
        pltpu.make_async_remote_copy(
            src_ref=src,
            dst_ref=dst,
            send_sem=self.sems.at[0, out_sem],
            recv_sem=self.sems.at[1, in_sem],
            device_id=to,
            device_id_type=MESH,
        ).start()
        self.sent[out_sem] = self.sent.get(out_sem, 0) + pieces

    def wait(self, way, sem, count):
        if count:
            like = self.terms.at[pl.ds(0, count * self.share)]
            pltpu.make_async_copy(like, like, self.sems.at[way, sem]).wait()

    def scatter(self):
        for k in range(1, self.layout.plane):
            to, device = self.peer_in_plane(k)
            self.send(self.terms.at[self.piece(to)], self.landed.at[self.piece(k - 1)], device, 0, 0)

    def cross(self):
        self.wait(1, 0, self.layout.plane - 1)
        total = self.terms[self.piece(self.place)]
        for k in range(self.layout.plane - 1):
            total = total + self.landed[self.piece(k)]
        self.held[...] = total
        for k in range(1, self.layout.line):
            self.send(self.held, self.crossed.at[self.piece(k - 1)], self.peer_in_line(k), 1, 1)

    def gather(self):
        self.wait(1, 1, self.layout.line - 1)
        mine = self.total.at[self.piece(self.place)]
        total = self.held[...]
        for k in range(self.layout.line - 1):
            total = total + self.crossed[self.piece(k)]
        mine[...] = total
        for k in range(1, self.layout.plane):
            self.send(mine, mine, self.peer_in_plane(k)[1], 2, 2)

    def relay(self):
        pass

    def forward(self):
        pass

    def finish(self):
        self.wait(1, 2, self.layout.plane - 1)

    def settle(self):
        for sem, count in sorted(self.sent.items()):
            self.wait(0, sem, count)


class PairedSum(Sum):
    def __init__(self, *args):
        super().__init__(*args)
        layout = self.layout
        self.core = lax.rem(self.group, layout.cores)
        self.chip = (self.group // layout.cores) * layout.width + lax.rem(self.dev, layout.width)
        self.place = self.core * layout.chips + self.chip

    def sibling(self):
        return self.group + 1 - 2 * self.core, self.dev

    def other_chip(self, k):
        layout = self.layout
        to = lax.rem(self.chip + k, layout.chips)
        group = (to // layout.width) * layout.cores + self.core
        return to, (group, self.plane * layout.width + lax.rem(to, layout.width))

    def share_of(self, core):
        chips = self.layout.chips
        return pl.ds(core * chips * self.share, chips * self.share)

    def scatter(self):
        chips = self.layout.chips
        src, dst = self.terms.at[self.share_of(1 - self.core)], self.landed.at[: chips * self.share]
        self.send(src, dst, self.sibling(), 0, 0, chips)

    def relay(self):
        chips = self.layout.chips
        self.wait(1, 0, chips)
        mine = self.share_of(self.core)
        self.terms[mine] = self.terms[mine] + self.landed[: chips * self.share]
        for k in range(1, chips):
            to, device = self.other_chip(k)
            src = self.terms.at[self.piece(self.core * chips + to)]
            self.send(src, self.landed.at[self.piece(chips + k - 1)], device, 1, 1)

    def cross(self):
        layout, chips = self.layout, self.layout.chips
        self.wait(1, 1, chips - 1)
        total = self.terms[self.piece(self.place)]
        for k in range(1, chips):
            total = total + self.landed[self.piece(chips + k - 1)]
        self.held[...] = total
        for k in range(1, layout.line):
            self.send(self.held, self.crossed.at[self.piece(k - 1)], self.peer_in_line(k), 2, 2)

    def gather(self):
        layout, chips = self.layout, self.layout.chips
        self.wait(1, 2, layout.line - 1)
        total = self.held[...]
        for k in range(layout.line - 1):
            total = total + self.crossed[self.piece(k)]
        mine = self.total.at[self.piece(self.place)]
        mine[...] = total
        for k in range(1, chips):
            self.send(mine, mine, self.other_chip(k)[1], 3, 3)

    def forward(self):
        chips = self.layout.chips
        self.wait(1, 3, chips - 1)
        mine = self.total.at[self.share_of(self.core)]
        self.send(mine, mine, self.sibling(), 4, 4, chips)

    def finish(self):
        self.wait(1, 4, self.layout.chips)


def sum_scratch(layout, share):
    tile = (SUB, LANES)
    return [
        pltpu.VMEM((layout.plane * share,) + tile, F32),
        pltpu.VMEM((max(layout.plane - 1, 1) * share,) + tile, F32),
        pltpu.VMEM((share,) + tile, F32),
        pltpu.VMEM((max(layout.line - 1, 1) * share,) + tile, F32),
        pltpu.VMEM((layout.plane * share,) + tile, F32),
        pltpu.SemaphoreType.DMA((2, 5)),
    ]


def to_tiles(ref, value):
    rows, columns = value.shape
    half = rows // SUB
    for c in range(columns // LANES):
        ref[c * half : (c + 1) * half] = value[:, c * LANES : (c + 1) * LANES].reshape(half, SUB, LANES)
    left = ref.shape[0] - half * (columns // LANES)
    if left:
        ref[ref.shape[0] - left :] = jnp.zeros((left, SUB, LANES), F32)


def from_tiles(ref, rows, columns):
    half = rows // SUB
    return jnp.concatenate(
        [ref[c * half : (c + 1) * half].reshape(rows, LANES) for c in range(columns // LANES)], axis=1
    )


def kernel(layout, n_group, owners_in, offsets_in, points_in, residual_in, change, *scratch):
    owners, offsets, points, residual, padded, flipped, tiles, loads = scratch[:8]
    sums = [scratch[8 + 6 * i : 14 + 6 * i] for i in range(2 * HALVES + 2)]
    group, dev = lax.axis_index("group"), lax.axis_index("dev")
    me = group * layout.n_dev + dev
    features, here_points = points.shape
    classes = residual.shape[0]
    rows = padded.shape[0]

    copies = [
        pltpu.make_async_copy(src, dst, loads.at[i])
        for i, (src, dst) in enumerate(
            [(points_in, points), (owners_in, owners), (offsets_in, offsets), (residual_in, residual)]
        )
    ]
    for copy in copies:
        copy.start()

    blocks_share = sums[0][2].shape[0]
    grads_share = sums[-1][2].shape[0]
    BlockSum = PairedSum if layout.cores == 2 else Sum
    at = (group, dev)
    spread = [BlockSum(layout, at, blocks_share, refs) for refs in sums[: 2 * HALVES]]
    grads = [Sum(layout, at, grads_share, refs) for refs in sums[2 * HALVES :]]
    left0, right0, left1, right1 = spread

    barrier = pltpu.get_barrier_semaphore()
    peers = [grads[0].peer_in_plane(k)[1] for k in range(1, layout.plane)]
    peers += [grads[0].peer_in_line(k) for k in range(1, layout.line)]
    for peer in peers:
        pl.semaphore_signal(barrier, inc=1, device_id=peer, device_id_type=MESH)

    def picker(step):
        first = jnp.where(owners[step] == me, offsets[step], 4 * here_points)
        row = lax.broadcasted_iota(jnp.int32, (BLOCK, here_points), 0)
        col = lax.broadcasted_iota(jnp.int32, (BLOCK, here_points), 1)
        return jnp.where(col == row + first, 1.0, 0.0).astype(jnp.bfloat16)

    def pick(index):
        chosen = picker(index // HALVES)
        at = index % HALVES * LANES
        chosen = chosen[at : at + LANES]
        dot = lambda a: lax.dot_general(a, chosen, (NT, ((), ())), preferred_element_type=F32)
        high, mid, low = pieces
        to_tiles(spread[index].terms, (dot(high) + dot(mid)) + dot(low))

    for copy in copies[:3]:
        copy.wait()
    pieces = split_three(points[...])
    pick(0)
    pl.semaphore_wait(barrier, len(peers))
    left0.scatter()
    pick(1)
    left0.relay()
    right0.scatter()
    cols = split_two(points[...].T)
    flipped[0], flipped[1] = cols
    right0.relay()
    left0.cross()
    cols = joined(cols)
    cols_norm = jnp.sum(cols * cols, axis=1, keepdims=True)
    right0.cross()
    pick(2)
    left1.scatter()
    for copy in copies[3:]:
        copy.wait()
    padded[...] = jnp.zeros_like(padded)
    padded[:classes] = residual[...]
    left0.gather()
    left1.relay()
    pick(3)
    right1.scatter()
    right0.gather()
    left1.cross()
    left0.forward()
    right1.relay()

    eye = (
        lax.broadcasted_iota(jnp.int32, (BLOCK, BLOCK), 0)
        == lax.broadcasted_iota(jnp.int32, (BLOCK, BLOCK), 1)
    ).astype(F32)

    def kernel_tile(left, left_norm, right):
        right = split_two(right)
        whole = joined(right)
        right_norm = jnp.sum(whole * whole, axis=0, keepdims=True)
        return jnp.exp(-(left_norm + right_norm - 2.0 * cross_dot(left, right)) / features)

    def half_block(index):
        return from_tiles(spread[index].total, features, LANES)

    def half_tile(index):
        spread[index].finish()
        at = index % HALVES * LANES
        tiles[index // HALVES, :, at : at + LANES] = kernel_tile(
            (flipped[0], flipped[1]), cols_norm, half_block(index)
        )

    class Inverse:
        def __init__(self, step):
            halves = [half_block(HALVES * step + h) for h in range(HALVES)]
            b = jnp.concatenate(halves, axis=1)
            rows = split_two(b.T)
            whole = joined(rows)
            gram = kernel_tile(rows, jnp.sum(whole * whole, axis=1, keepdims=True), b) + ridge * eye
            top = jnp.max(jnp.sum(gram, axis=1, keepdims=True), axis=0, keepdims=True)
            centre = 2.0 / (ridge + top)
            err = (top - ridge) / (top + ridge)
            gain = 2.0 / (2.0 - err * err)
            self.gram = gram
            self.value = (gain * centre) * (2.0 * eye - centre * gram)
            self.err = err * err / (2.0 - err * err)

        def gain(self):
            err = self.err
            self.err = err * err / (2.0 - err * err)
            return 2.0 / (2.0 - err * err)

        def rough(self):
            near = self.value.astype(jnp.bfloat16)
            rest = eye - low_dot(self.gram, near)
            self.value = self.gain() * (near.astype(F32) + low_dot(near, rest))

        def fine(self):
            rest = eye - split_dot(self.gram, self.value)
            self.value = self.gain() * (self.value + low_dot(self.value, rest))

        def polish(self):
            rest = eye - exact_dot(self.gram, self.value, NN)
            self.value = self.value + low_dot(self.value, rest)

    def sum_grad(step):
        to_tiles(grads[step].terms, exact_dot(padded[...], tiles[step], NN))
        grads[step].scatter()

    def make_delta(step, inverse):
        grad = from_tiles(grads[step].total, rows, BLOCK)
        square = jnp.sum(jnp.sum(grad * grad, axis=1, keepdims=True), axis=0, keepdims=True)
        scale = step_norm / jnp.sqrt(square / (classes * BLOCK) + 1e-06)
        return scale * exact_dot(grad, inverse, NN)

    def credit(step, delta):
        chosen = picker(step)
        high, mid, low = split_three(delta)
        dot = lambda a: jnp.dot(a, chosen, preferred_element_type=F32)
        return ((dot(high) + dot(mid)) + dot(low))[:classes]

    half_tile(0)
    right0.forward()
    right1.cross()
    half_tile(1)
    sum_grad(0)
    inverse = Inverse(0)
    inverse.rough()
    grads[0].cross()
    left1.gather()
    right1.gather()
    inverse.rough()
    inverse.rough()
    inverse.fine()
    grads[0].gather()
    left1.forward()
    right1.forward()
    inverse.fine()
    half_tile(2)
    half_tile(3)
    inverse.polish()
    grads[0].finish()
    delta = make_delta(0, inverse.value)
    step = split_dot(delta, tiles[0], NT)
    padded[...] = padded[...] - step
    sum_grad(1)
    change[0] = step[:classes]
    change[1] = credit(0, delta)
    inverse = Inverse(1)
    inverse.rough()
    grads[1].cross()
    for each in spread:
        each.settle()
    grads[0].settle()
    inverse.rough()
    inverse.rough()
    inverse.fine()
    grads[1].gather()
    inverse.fine()
    inverse.polish()
    grads[1].finish()
    delta = make_delta(1, inverse.value)
    change[0] = change[0] + split_dot(delta, tiles[1], NT)[:classes]
    change[1] = change[1] + credit(1, delta)
    grads[1].settle()


def solution(mesh):
    n_group, n_dev = mesh.shape["group"], mesh.shape["dev"]
    layout = Layout(n_group, n_dev)

    def body(points, residual, coeffs, owners, offsets):
        features, here = points.shape
        classes = residual.shape[0]
        rows = -(-classes // SUB) * SUB
        blocks_share = layout.share(features // SUB)
        grads_share = layout.share(rows // SUB * HALVES)
        vmem = pl.BlockSpec(memory_space=pltpu.VMEM)
        outside = pl.BlockSpec(memory_space=pltpu.HBM)
        change = pl.pallas_call(
            functools.partial(kernel, layout, n_group),
            out_shape=jax.ShapeDtypeStruct((2,) + residual.shape, F32),
            in_specs=[outside] * 4,
            out_specs=vmem,
            scratch_shapes=[
                pltpu.SMEM(owners.shape, jnp.int32),
                pltpu.SMEM(offsets.shape, jnp.int32),
                pltpu.VMEM(points.shape, F32),
                pltpu.VMEM(residual.shape, F32),
                pltpu.VMEM((rows, here), F32),
                pltpu.VMEM((2, here, features), jnp.bfloat16),
                pltpu.VMEM((2, here, BLOCK), F32),
                pltpu.SemaphoreType.DMA((4,)),
            ]
            + sum_scratch(layout, blocks_share) * (2 * HALVES)
            + sum_scratch(layout, grads_share) * 2,
            compiler_params=pltpu.CompilerParams(
                collective_id=0, has_side_effects=True, vmem_limit_bytes=60 * 1024 * 1024
            ),
        )(owners, offsets, points, residual)
        return residual - change[0], coeffs + change[1]

    split = P(None, ("group", "dev"))
    return jax.shard_map(
        body,
        mesh=mesh,
        in_specs=(split, split, split, P(), P()),
        out_specs=(split, split),
        check_vma=False,
    )
```

```python
import functools

import jax
import jax.numpy as jnp
from jax import lax
from jax.experimental import pallas as pl
from jax.experimental.pallas import tpu as pltpu
from jax.sharding import PartitionSpec as P

BLOCK = 256
LANES = 128
HALVES = BLOCK // LANES
SUB = 8

ridge = 2.0
step_norm = 1.5

MESH = pl.DeviceIdType.MESH
F32 = jnp.float32


def exact_dot(a, b, dims):
    return lax.dot_general(
        a, b, (dims, ((), ())), precision=lax.Precision.HIGHEST, preferred_element_type=F32
    )


NN = ((1,), (0,))
NT = ((1,), (1,))


def low_dot(a, b):
    return jnp.dot(a.astype(jnp.bfloat16), b.astype(jnp.bfloat16), preferred_element_type=F32)


def split_dot(a, b, dims=NN):
    ah, bh = a.astype(jnp.bfloat16), b.astype(jnp.bfloat16)
    al = (a - ah.astype(F32)).astype(jnp.bfloat16)
    bl = (b - bh.astype(F32)).astype(jnp.bfloat16)
    dot = lambda u, v: lax.dot_general(u, v, (dims, ((), ())), preferred_element_type=F32)
    return dot(ah, bh) + (dot(ah, bl) + dot(al, bh))


def split_two(x):
    high = x.astype(jnp.bfloat16)
    return high, (x - high.astype(F32)).astype(jnp.bfloat16)


def joined(parts):
    return parts[0].astype(F32) + parts[1].astype(F32)


def cross_dot(left, right):
    width = right[0].shape[1]
    both = jnp.concatenate(right, axis=1)
    out = jnp.dot(left[0], both, preferred_element_type=F32)
    out = out + jnp.dot(left[1], both, preferred_element_type=F32)
    return out[:, :width] + out[:, width:]


def split_three(x):
    high = x.astype(jnp.bfloat16)
    rest = x - high.astype(F32)
    mid = rest.astype(jnp.bfloat16)
    return high, mid, (rest - mid.astype(F32)).astype(jnp.bfloat16)


def line_width(n_dev):
    width = 1
    while n_dev % (2 * width) == 0 and 4 * width * width <= n_dev:
        width *= 2
    return width


class Layout:
    def __init__(self, n_group, n_dev):
        self.n_dev = n_dev
        self.width = line_width(n_dev)
        self.plane = n_group * self.width
        self.line = n_dev // self.width
        self.cores = 2 if n_group % 2 == 0 else 1
        self.chips = self.plane // self.cores

    def share(self, tiles):
        return -(-tiles // self.plane)


class Sum:
    def __init__(self, layout, at, share, refs):
        self.layout, self.share = layout, share
        self.group, self.dev = at
        self.terms, self.landed, self.held, self.crossed, self.total, self.sems = refs
        self.place = self.group * layout.width + lax.rem(self.dev, layout.width)
        self.plane = self.dev // layout.width
        self.sent = {}

    def peer_in_plane(self, k):
        to = lax.rem(self.place + k, self.layout.plane)
        width = self.layout.width
        return to, (to // width, self.plane * width + lax.rem(to, width))

    def peer_in_line(self, k):
        to = lax.rem(self.plane + k, self.layout.line)
        width = self.layout.width
        return self.group, to * width + lax.rem(self.dev, width)

    def peers(self):
        layout = self.layout
        plane = [self.peer_in_plane(k)[1] for k in range(1, layout.plane)]
        return plane + [self.peer_in_line(k) for k in range(1, layout.line)]

    def piece(self, index):
        return pl.ds(index * self.share, self.share)

    def send(self, src, dst, to, out_sem, in_sem, pieces=1):
        pltpu.make_async_remote_copy(
            src_ref=src,
            dst_ref=dst,
            send_sem=self.sems.at[0, out_sem],
            recv_sem=self.sems.at[1, in_sem],
            device_id=to,
            device_id_type=MESH,
        ).start()
        self.sent[out_sem] = self.sent.get(out_sem, 0) + pieces

    def wait(self, way, sem, count):
        if count:
            like = self.terms.at[pl.ds(0, count * self.share)]
            pltpu.make_async_copy(like, like, self.sems.at[way, sem]).wait()

    def scatter(self):
        for k in range(1, self.layout.plane):
            to, device = self.peer_in_plane(k)
            self.send(self.terms.at[self.piece(to)], self.landed.at[self.piece(k - 1)], device, 0, 0)

    def cross(self):
        self.wait(1, 0, self.layout.plane - 1)
        total = self.terms[self.piece(self.place)]
        for k in range(self.layout.plane - 1):
            total = total + self.landed[self.piece(k)]
        self.held[...] = total
        for k in range(1, self.layout.line):
            self.send(self.held, self.crossed.at[self.piece(k - 1)], self.peer_in_line(k), 1, 1)

    def gather(self):
        self.wait(1, 1, self.layout.line - 1)
        mine = self.total.at[self.piece(self.place)]
        total = self.held[...]
        for k in range(self.layout.line - 1):
            total = total + self.crossed[self.piece(k)]
        mine[...] = total
        for k in range(1, self.layout.plane):
            self.send(mine, mine, self.peer_in_plane(k)[1], 2, 2)

    def relay(self):
        pass

    def forward(self):
        pass

    def finish(self):
        self.wait(1, 2, self.layout.plane - 1)

    def settle(self):
        for sem, count in sorted(self.sent.items()):
            self.wait(0, sem, count)


class PairedSum(Sum):
    def __init__(self, *args):
        super().__init__(*args)
        layout = self.layout
        self.core = lax.rem(self.group, layout.cores)
        self.chip = (self.group // layout.cores) * layout.width + lax.rem(self.dev, layout.width)
        self.place = self.core * layout.chips + self.chip

    def sibling(self):
        return self.group + 1 - 2 * self.core, self.dev

    def other_chip(self, k):
        layout = self.layout
        to = lax.rem(self.chip + k, layout.chips)
        group = (to // layout.width) * layout.cores + self.core
        return to, (group, self.plane * layout.width + lax.rem(to, layout.width))

    def peers(self):
        layout = self.layout
        chips = [self.other_chip(k)[1] for k in range(1, layout.chips)]
        return [self.sibling()] + chips + [self.peer_in_line(k) for k in range(1, layout.line)]

    def share_of(self, core):
        chips = self.layout.chips
        return pl.ds(core * chips * self.share, chips * self.share)

    def scatter(self):
        chips = self.layout.chips
        src, dst = self.terms.at[self.share_of(1 - self.core)], self.landed.at[: chips * self.share]
        self.send(src, dst, self.sibling(), 0, 0, chips)

    def relay(self):
        chips = self.layout.chips
        self.wait(1, 0, chips)
        mine = self.share_of(self.core)
        self.terms[mine] = self.terms[mine] + self.landed[: chips * self.share]
        for k in range(1, chips):
            to, device = self.other_chip(k)
            src = self.terms.at[self.piece(self.core * chips + to)]
            self.send(src, self.landed.at[self.piece(chips + k - 1)], device, 1, 1)

    def cross(self):
        layout, chips = self.layout, self.layout.chips
        self.wait(1, 1, chips - 1)
        total = self.terms[self.piece(self.place)]
        for k in range(1, chips):
            total = total + self.landed[self.piece(chips + k - 1)]
        self.held[...] = total
        for k in range(1, layout.line):
            self.send(self.held, self.crossed.at[self.piece(k - 1)], self.peer_in_line(k), 2, 2)

    def gather(self):
        layout, chips = self.layout, self.layout.chips
        self.wait(1, 2, layout.line - 1)
        total = self.held[...]
        for k in range(layout.line - 1):
            total = total + self.crossed[self.piece(k)]
        mine = self.total.at[self.piece(self.place)]
        mine[...] = total
        for k in range(1, chips):
            self.send(mine, mine, self.other_chip(k)[1], 3, 3)

    def forward(self):
        chips = self.layout.chips
        self.wait(1, 3, chips - 1)
        mine = self.total.at[self.share_of(self.core)]
        self.send(mine, mine, self.sibling(), 4, 4, chips)

    def finish(self):
        self.wait(1, 4, self.layout.chips)


def sum_scratch(layout, share):
    tile = (SUB, LANES)
    return [
        pltpu.VMEM((layout.plane * share,) + tile, F32),
        pltpu.VMEM((max(layout.plane - 1, 1) * share,) + tile, F32),
        pltpu.VMEM((share,) + tile, F32),
        pltpu.VMEM((max(layout.line - 1, 1) * share,) + tile, F32),
        pltpu.VMEM((layout.plane * share,) + tile, F32),
        pltpu.SemaphoreType.DMA((2, 5)),
    ]


def to_tiles(ref, value):
    rows, columns = value.shape
    half = rows // SUB
    for c in range(columns // LANES):
        ref[c * half : (c + 1) * half] = value[:, c * LANES : (c + 1) * LANES].reshape(half, SUB, LANES)
    left = ref.shape[0] - half * (columns // LANES)
    if left:
        ref[ref.shape[0] - left :] = jnp.zeros((left, SUB, LANES), F32)


def from_tiles(ref, rows, columns):
    half = rows // SUB
    return jnp.concatenate(
        [ref[c * half : (c + 1) * half].reshape(rows, LANES) for c in range(columns // LANES)], axis=1
    )


def kernel(layout, n_group, owners_in, offsets_in, points_in, residual_in, change, *scratch):
    owners, offsets, points, residual, padded, flipped, tiles, loads = scratch[:8]
    sums = [scratch[8 + 6 * i : 14 + 6 * i] for i in range(2 * HALVES + 2)]
    group, dev = lax.axis_index("group"), lax.axis_index("dev")
    me = group * layout.n_dev + dev
    features, here_points = points.shape
    classes = residual.shape[0]
    rows = padded.shape[0]

    copies = [
        pltpu.make_async_copy(src, dst, loads.at[i])
        for i, (src, dst) in enumerate(
            [(points_in, points), (owners_in, owners), (offsets_in, offsets), (residual_in, residual)]
        )
    ]
    for copy in copies:
        copy.start()

    blocks_share = sums[0][2].shape[0]
    grads_share = sums[-1][2].shape[0]
    BlockSum = PairedSum if layout.cores == 2 else Sum
    at = (group, dev)
    spread = [BlockSum(layout, at, blocks_share, refs) for refs in sums[: 2 * HALVES]]
    grads = [BlockSum(layout, at, grads_share, refs) for refs in sums[2 * HALVES :]]
    left0, right0, left1, right1 = spread

    barrier = pltpu.get_barrier_semaphore()
    peers = grads[0].peers()
    for peer in peers:
        pl.semaphore_signal(barrier, inc=1, device_id=peer, device_id_type=MESH)

    def picker(step):
        first = jnp.where(owners[step] == me, offsets[step], 4 * here_points)
        row = lax.broadcasted_iota(jnp.int32, (BLOCK, here_points), 0)
        col = lax.broadcasted_iota(jnp.int32, (BLOCK, here_points), 1)
        return jnp.where(col == row + first, 1.0, 0.0).astype(jnp.bfloat16)

    def pick(index):
        chosen = picker(index // HALVES)
        at = index % HALVES * LANES
        chosen = chosen[at : at + LANES]
        dot = lambda a: lax.dot_general(a, chosen, (NT, ((), ())), preferred_element_type=F32)
        high, mid, low = pieces
        to_tiles(spread[index].terms, (dot(high) + dot(mid)) + dot(low))

    for copy in copies[:3]:
        copy.wait()
    pieces = split_three(points[...])
    pick(0)
    pl.semaphore_wait(barrier, len(peers))
    left0.scatter()
    pick(1)
    left0.relay()
    right0.scatter()
    cols = split_two(points[...].T)
    flipped[0], flipped[1] = cols
    right0.relay()
    left0.cross()
    cols = joined(cols)
    cols_norm = jnp.sum(cols * cols, axis=1, keepdims=True)
    right0.cross()
    pick(2)
    left1.scatter()
    for copy in copies[3:]:
        copy.wait()
    padded[...] = jnp.zeros_like(padded)
    padded[:classes] = residual[...]
    left0.gather()
    left1.relay()
    pick(3)
    right1.scatter()
    right0.gather()
    left1.cross()
    left0.forward()
    right1.relay()

    eye = (
        lax.broadcasted_iota(jnp.int32, (BLOCK, BLOCK), 0)
        == lax.broadcasted_iota(jnp.int32, (BLOCK, BLOCK), 1)
    ).astype(F32)

    def kernel_tile(left, left_norm, right):
        right = split_two(right)
        whole = joined(right)
        right_norm = jnp.sum(whole * whole, axis=0, keepdims=True)
        return jnp.exp(-(left_norm + right_norm - 2.0 * cross_dot(left, right)) / features)

    def half_block(index):
        return from_tiles(spread[index].total, features, LANES)

    def half_tile(index):
        spread[index].finish()
        at = index % HALVES * LANES
        tiles[index // HALVES, :, at : at + LANES] = kernel_tile(
            (flipped[0], flipped[1]), cols_norm, half_block(index)
        )

    class Inverse:
        def __init__(self, step):
            halves = [half_block(HALVES * step + h) for h in range(HALVES)]
            b = jnp.concatenate(halves, axis=1)
            rows = split_two(b.T)
            whole = joined(rows)
            gram = kernel_tile(rows, jnp.sum(whole * whole, axis=1, keepdims=True), b) + ridge * eye
            top = jnp.max(jnp.sum(gram, axis=1, keepdims=True), axis=0, keepdims=True)
            centre = 2.0 / (ridge + top)
            err = (top - ridge) / (top + ridge)
            gain = 2.0 / (2.0 - err * err)
            self.gram = gram
            self.value = (gain * centre) * (2.0 * eye - centre * gram)
            self.err = err * err / (2.0 - err * err)

        def gain(self):
            err = self.err
            self.err = err * err / (2.0 - err * err)
            return 2.0 / (2.0 - err * err)

        def rough(self):
            near = self.value.astype(jnp.bfloat16)
            rest = eye - low_dot(self.gram, near)
            self.value = self.gain() * (near.astype(F32) + low_dot(near, rest))

        def fine(self):
            rest = eye - split_dot(self.gram, self.value)
            self.value = self.gain() * (self.value + low_dot(self.value, rest))

        def polish(self):
            rest = eye - exact_dot(self.gram, self.value, NN)
            self.value = self.value + low_dot(self.value, rest)

    def sum_grad(step):
        to_tiles(grads[step].terms, exact_dot(padded[...], tiles[step], NN))
        grads[step].scatter()

    def make_delta(step, inverse):
        grad = from_tiles(grads[step].total, rows, BLOCK)
        square = jnp.sum(jnp.sum(grad * grad, axis=1, keepdims=True), axis=0, keepdims=True)
        scale = step_norm / jnp.sqrt(square / (classes * BLOCK) + 1e-06)
        return scale * exact_dot(grad, inverse, NN)

    def credit(step, delta):
        chosen = picker(step)
        high, mid, low = split_three(delta)
        dot = lambda a: jnp.dot(a, chosen, preferred_element_type=F32)
        return ((dot(high) + dot(mid)) + dot(low))[:classes]

    half_tile(0)
    right0.forward()
    right1.cross()
    half_tile(1)
    sum_grad(0)
    inverse = Inverse(0)
    grads[0].relay()
    inverse.rough()
    grads[0].cross()
    left1.gather()
    right1.gather()
    inverse.rough()
    inverse.rough()
    inverse.fine()
    grads[0].gather()
    left1.forward()
    right1.forward()
    inverse.fine()
    half_tile(2)
    grads[0].forward()
    half_tile(3)
    inverse.polish()
    grads[0].finish()
    delta = make_delta(0, inverse.value)
    step = split_dot(delta, tiles[0], NT)
    padded[...] = padded[...] - step
    sum_grad(1)
    change[0] = step[:classes]
    change[1] = credit(0, delta)
    inverse = Inverse(1)
    grads[1].relay()
    inverse.rough()
    grads[1].cross()
    for each in spread:
        each.settle()
    grads[0].settle()
    inverse.rough()
    inverse.rough()
    inverse.fine()
    grads[1].gather()
    inverse.fine()
    inverse.polish()
    grads[1].forward()
    grads[1].finish()
    delta = make_delta(1, inverse.value)
    change[0] = change[0] + split_dot(delta, tiles[1], NT)[:classes]
    change[1] = change[1] + credit(1, delta)
    grads[1].settle()


def solution(mesh):
    n_group, n_dev = mesh.shape["group"], mesh.shape["dev"]
    layout = Layout(n_group, n_dev)

    def body(points, residual, coeffs, owners, offsets):
        features, here = points.shape
        classes = residual.shape[0]
        rows = -(-classes // SUB) * SUB
        blocks_share = layout.share(features // SUB)
        grads_share = layout.share(rows // SUB * HALVES)
        vmem = pl.BlockSpec(memory_space=pltpu.VMEM)
        outside = pl.BlockSpec(memory_space=pltpu.HBM)
        change = pl.pallas_call(
            functools.partial(kernel, layout, n_group),
            out_shape=jax.ShapeDtypeStruct((2,) + residual.shape, F32),
            in_specs=[outside] * 4,
            out_specs=vmem,
            scratch_shapes=[
                pltpu.SMEM(owners.shape, jnp.int32),
                pltpu.SMEM(offsets.shape, jnp.int32),
                pltpu.VMEM(points.shape, F32),
                pltpu.VMEM(residual.shape, F32),
                pltpu.VMEM((rows, here), F32),
                pltpu.VMEM((2, here, features), jnp.bfloat16),
                pltpu.VMEM((2, here, BLOCK), F32),
                pltpu.SemaphoreType.DMA((4,)),
            ]
            + sum_scratch(layout, blocks_share) * (2 * HALVES)
            + sum_scratch(layout, grads_share) * 2,
            compiler_params=pltpu.CompilerParams(
                collective_id=0, has_side_effects=True, vmem_limit_bytes=60 * 1024 * 1024
            ),
        )(owners, offsets, points, residual)
        return residual - change[0], coeffs + change[1]

    split = P(None, ("group", "dev"))
    return jax.shard_map(
        body,
        mesh=mesh,
        in_specs=(split, split, split, P(), P()),
        out_specs=(split, split),
        check_vma=False,
    )
```

```python
import functools

import jax
import jax.numpy as jnp
from jax import lax
from jax.experimental import pallas as pl
from jax.experimental.pallas import tpu as pltpu
from jax.sharding import PartitionSpec as P

BLOCK = 256
LANES = 128
HALVES = BLOCK // LANES
SUB = 8

ridge = 2.0
step_norm = 1.5

MESH = pl.DeviceIdType.MESH
F32 = jnp.float32


def exact_dot(a, b, dims):
    return lax.dot_general(
        a, b, (dims, ((), ())), precision=lax.Precision.HIGHEST, preferred_element_type=F32
    )


NN = ((1,), (0,))
NT = ((1,), (1,))


def low_dot(a, b):
    return jnp.dot(a.astype(jnp.bfloat16), b.astype(jnp.bfloat16), preferred_element_type=F32)


def split_dot(a, b, dims=NN):
    ah, bh = a.astype(jnp.bfloat16), b.astype(jnp.bfloat16)
    al = (a - ah.astype(F32)).astype(jnp.bfloat16)
    bl = (b - bh.astype(F32)).astype(jnp.bfloat16)
    dot = lambda u, v: lax.dot_general(u, v, (dims, ((), ())), preferred_element_type=F32)
    return dot(ah, bh) + (dot(ah, bl) + dot(al, bh))


def split_two(x):
    high = x.astype(jnp.bfloat16)
    return high, (x - high.astype(F32)).astype(jnp.bfloat16)


def joined(parts):
    return parts[0].astype(F32) + parts[1].astype(F32)


def cross_dot(left, right):
    width = right[0].shape[1]
    both = jnp.concatenate(right, axis=1)
    out = jnp.dot(left[0], both, preferred_element_type=F32)
    out = out + jnp.dot(left[1], both, preferred_element_type=F32)
    return out[:, :width] + out[:, width:]


def split_three(x):
    high = x.astype(jnp.bfloat16)
    rest = x - high.astype(F32)
    mid = rest.astype(jnp.bfloat16)
    return high, mid, (rest - mid.astype(F32)).astype(jnp.bfloat16)


def line_width(n_dev):
    width = 1
    while n_dev % (2 * width) == 0 and 4 * width * width <= n_dev:
        width *= 2
    return width


class Layout:
    def __init__(self, n_group, n_dev):
        self.n_dev = n_dev
        self.width = line_width(n_dev)
        self.plane = n_group * self.width
        self.line = n_dev // self.width
        self.cores = 2 if n_group % 2 == 0 else 1
        self.chips = self.plane // self.cores

    def share(self, tiles):
        return -(-tiles // self.plane)


class Sum:
    def __init__(self, layout, at, share, refs):
        self.layout, self.share = layout, share
        self.group, self.dev = at
        self.terms, self.landed, self.held, self.crossed, self.total, self.sems = refs
        self.place = self.group * layout.width + lax.rem(self.dev, layout.width)
        self.plane = self.dev // layout.width
        self.sent = {}

    def peer_in_plane(self, k):
        to = lax.rem(self.place + k, self.layout.plane)
        width = self.layout.width
        return to, (to // width, self.plane * width + lax.rem(to, width))

    def peer_in_line(self, k):
        to = lax.rem(self.plane + k, self.layout.line)
        width = self.layout.width
        return self.group, to * width + lax.rem(self.dev, width)

    def piece(self, index):
        return pl.ds(index * self.share, self.share)

    def send(self, src, dst, to, out_sem, in_sem, pieces=1):
        pltpu.make_async_remote_copy(
            src_ref=src,
            dst_ref=dst,
            send_sem=self.sems.at[0, out_sem],
            recv_sem=self.sems.at[1, in_sem],
            device_id=to,
            device_id_type=MESH,
        ).start()
        self.sent[out_sem] = self.sent.get(out_sem, 0) + pieces

    def wait(self, way, sem, count):
        if count:
            like = self.terms.at[pl.ds(0, count * self.share)]
            pltpu.make_async_copy(like, like, self.sems.at[way, sem]).wait()

    def scatter(self):
        for k in range(1, self.layout.plane):
            to, device = self.peer_in_plane(k)
            self.send(self.terms.at[self.piece(to)], self.landed.at[self.piece(k - 1)], device, 0, 0)

    def cross(self):
        self.wait(1, 0, self.layout.plane - 1)
        total = self.terms[self.piece(self.place)]
        for k in range(self.layout.plane - 1):
            total = total + self.landed[self.piece(k)]
        self.held[...] = total
        for k in range(1, self.layout.line):
            self.send(self.held, self.crossed.at[self.piece(k - 1)], self.peer_in_line(k), 1, 1)

    def gather(self):
        self.wait(1, 1, self.layout.line - 1)
        mine = self.total.at[self.piece(self.place)]
        total = self.held[...]
        for k in range(self.layout.line - 1):
            total = total + self.crossed[self.piece(k)]
        mine[...] = total
        for k in range(1, self.layout.plane):
            self.send(mine, mine, self.peer_in_plane(k)[1], 2, 2)

    def relay(self):
        pass

    def forward(self):
        pass

    def finish(self):
        self.wait(1, 2, self.layout.plane - 1)

    def settle(self):
        for sem, count in sorted(self.sent.items()):
            self.wait(0, sem, count)


class PairedSum(Sum):
    def __init__(self, *args):
        super().__init__(*args)
        layout = self.layout
        self.core = lax.rem(self.group, layout.cores)
        self.chip = (self.group // layout.cores) * layout.width + lax.rem(self.dev, layout.width)
        self.place = self.core * layout.chips + self.chip

    def sibling(self):
        return self.group + 1 - 2 * self.core, self.dev

    def other_chip(self, k):
        layout = self.layout
        to = lax.rem(self.chip + k, layout.chips)
        group = (to // layout.width) * layout.cores + self.core
        return to, (group, self.plane * layout.width + lax.rem(to, layout.width))

    def share_of(self, core):
        chips = self.layout.chips
        return pl.ds(core * chips * self.share, chips * self.share)

    def scatter(self):
        chips = self.layout.chips
        src, dst = self.terms.at[self.share_of(1 - self.core)], self.landed.at[: chips * self.share]
        self.send(src, dst, self.sibling(), 0, 0, chips)

    def relay(self):
        chips = self.layout.chips
        self.wait(1, 0, chips)
        mine = self.share_of(self.core)
        self.terms[mine] = self.terms[mine] + self.landed[: chips * self.share]
        for k in range(1, chips):
            to, device = self.other_chip(k)
            src = self.terms.at[self.piece(self.core * chips + to)]
            self.send(src, self.landed.at[self.piece(chips + k - 1)], device, 1, 1)

    def cross(self):
        layout, chips = self.layout, self.layout.chips
        self.wait(1, 1, chips - 1)
        total = self.terms[self.piece(self.place)]
        for k in range(1, chips):
            total = total + self.landed[self.piece(chips + k - 1)]
        self.held[...] = total
        for k in range(1, layout.line):
            self.send(self.held, self.crossed.at[self.piece(k - 1)], self.peer_in_line(k), 2, 2)

    def gather(self):
        layout, chips = self.layout, self.layout.chips
        self.wait(1, 2, layout.line - 1)
        total = self.held[...]
        for k in range(layout.line - 1):
            total = total + self.crossed[self.piece(k)]
        mine = self.total.at[self.piece(self.place)]
        mine[...] = total
        for k in range(1, chips):
            self.send(mine, mine, self.other_chip(k)[1], 3, 3)

    def forward(self):
        chips = self.layout.chips
        self.wait(1, 3, chips - 1)
        mine = self.total.at[self.share_of(self.core)]
        self.send(mine, mine, self.sibling(), 4, 4, chips)

    def finish(self):
        self.wait(1, 4, self.layout.chips)


def sum_scratch(layout, share):
    tile = (SUB, LANES)
    return [
        pltpu.VMEM((layout.plane * share,) + tile, F32),
        pltpu.VMEM((max(layout.plane - 1, 1) * share,) + tile, F32),
        pltpu.VMEM((share,) + tile, F32),
        pltpu.VMEM((max(layout.line - 1, 1) * share,) + tile, F32),
        pltpu.VMEM((layout.plane * share,) + tile, F32),
        pltpu.SemaphoreType.DMA((2, 5)),
    ]


def to_tiles(ref, value):
    rows, columns = value.shape
    half = rows // SUB
    for c in range(columns // LANES):
        ref[c * half : (c + 1) * half] = value[:, c * LANES : (c + 1) * LANES].reshape(half, SUB, LANES)
    left = ref.shape[0] - half * (columns // LANES)
    if left:
        ref[ref.shape[0] - left :] = jnp.zeros((left, SUB, LANES), F32)


def from_tiles(ref, rows, columns):
    half = rows // SUB
    return jnp.concatenate(
        [ref[c * half : (c + 1) * half].reshape(rows, LANES) for c in range(columns // LANES)], axis=1
    )


def kernel(layout, n_group, owners_in, offsets_in, points_in, residual_in, change, *scratch):
    owners, offsets, points, residual, padded, flipped, tiles, loads = scratch[:8]
    sums = [scratch[8 + 6 * i : 14 + 6 * i] for i in range(HALVES + 3)]
    group, dev = lax.axis_index("group"), lax.axis_index("dev")
    me = group * layout.n_dev + dev
    features, here_points = points.shape
    classes = residual.shape[0]
    rows = padded.shape[0]

    copies = [
        pltpu.make_async_copy(src, dst, loads.at[i])
        for i, (src, dst) in enumerate(
            [(points_in, points), (owners_in, owners), (offsets_in, offsets), (residual_in, residual)]
        )
    ]
    for copy in copies:
        copy.start()

    BlockSum = PairedSum if layout.cores == 2 else Sum
    at = (group, dev)
    spread = [BlockSum(layout, at, refs[2].shape[0], refs) for refs in sums[: HALVES + 1]]
    grads = [Sum(layout, at, refs[2].shape[0], refs) for refs in sums[HALVES + 1 :]]
    left0, right0, second = spread

    barrier = pltpu.get_barrier_semaphore()
    peers = [grads[0].peer_in_plane(k)[1] for k in range(1, layout.plane)]
    peers += [grads[0].peer_in_line(k) for k in range(1, layout.line)]
    for peer in peers:
        pl.semaphore_signal(barrier, inc=1, device_id=peer, device_id_type=MESH)

    def picker(step):
        first = jnp.where(owners[step] == me, offsets[step], 4 * here_points)
        row = lax.broadcasted_iota(jnp.int32, (BLOCK, here_points), 0)
        col = lax.broadcasted_iota(jnp.int32, (BLOCK, here_points), 1)
        return jnp.where(col == row + first, 1.0, 0.0).astype(jnp.bfloat16)

    def pick(target, chosen):
        dot = lambda a: lax.dot_general(a, chosen, (NT, ((), ())), preferred_element_type=F32)
        high, mid, low = pieces
        to_tiles(target.terms, (dot(high) + dot(mid)) + dot(low))

    for copy in copies[:3]:
        copy.wait()
    pieces = split_three(points[...])
    chosen = picker(0)
    pick(left0, chosen[:LANES])
    pl.semaphore_wait(barrier, len(peers))
    left0.scatter()
    pick(right0, chosen[LANES:])
    left0.relay()
    right0.scatter()
    cols = split_two(points[...].T)
    flipped[0], flipped[1] = cols
    right0.relay()
    left0.cross()
    cols = joined(cols)
    cols_norm = jnp.sum(cols * cols, axis=1, keepdims=True)
    right0.cross()
    pick(second, picker(1))
    second.scatter()
    for copy in copies[3:]:
        copy.wait()
    padded[...] = jnp.zeros_like(padded)
    padded[:classes] = residual[...]
    left0.gather()
    second.relay()
    right0.gather()
    left0.forward()

    eye = (
        lax.broadcasted_iota(jnp.int32, (BLOCK, BLOCK), 0)
        == lax.broadcasted_iota(jnp.int32, (BLOCK, BLOCK), 1)
    ).astype(F32)

    def kernel_tile(left, left_norm, right):
        right = split_two(right)
        whole = joined(right)
        right_norm = jnp.sum(whole * whole, axis=0, keepdims=True)
        return jnp.exp(-(left_norm + right_norm - 2.0 * cross_dot(left, right)) / features)

    def block(step):
        if step:
            return from_tiles(second.total, features, BLOCK)
        halves = [from_tiles(half.total, features, LANES) for half in (left0, right0)]
        return jnp.concatenate(halves, axis=1)

    def make_tile(step, source, first, width):
        source.finish()
        tiles[step, :, first : first + width] = kernel_tile(
            (flipped[0], flipped[1]), cols_norm, from_tiles(source.total, features, width)
        )

    class Inverse:
        def __init__(self, step):
            b = block(step)
            rows = split_two(b.T)
            whole = joined(rows)
            gram = kernel_tile(rows, jnp.sum(whole * whole, axis=1, keepdims=True), b) + ridge * eye
            top = jnp.max(jnp.sum(gram, axis=1, keepdims=True), axis=0, keepdims=True)
            centre = 2.0 / (ridge + top)
            err = (top - ridge) / (top + ridge)
            gain = 2.0 / (2.0 - err * err)
            self.gram = gram
            self.value = (gain * centre) * (2.0 * eye - centre * gram)
            self.err = err * err / (2.0 - err * err)

        def gain(self):
            err = self.err
            self.err = err * err / (2.0 - err * err)
            return 2.0 / (2.0 - err * err)

        def rough(self):
            near = self.value.astype(jnp.bfloat16)
            rest = eye - low_dot(self.gram, near)
            self.value = self.gain() * (near.astype(F32) + low_dot(near, rest))

        def fine(self):
            rest = eye - split_dot(self.gram, self.value)
            self.value = self.gain() * (self.value + low_dot(self.value, rest))

        def polish(self):
            rest = eye - exact_dot(self.gram, self.value, NN)
            self.value = self.value + low_dot(self.value, rest)

    def sum_grad(step):
        to_tiles(grads[step].terms, exact_dot(padded[...], tiles[step], NN))
        grads[step].scatter()

    def make_delta(step, inverse):
        grad = from_tiles(grads[step].total, rows, BLOCK)
        square = jnp.sum(jnp.sum(grad * grad, axis=1, keepdims=True), axis=0, keepdims=True)
        scale = step_norm / jnp.sqrt(square / (classes * BLOCK) + 1e-06)
        return scale * exact_dot(grad, inverse, NN)

    def credit(step, delta):
        chosen = picker(step)
        high, mid, low = split_three(delta)
        dot = lambda a: jnp.dot(a, chosen, preferred_element_type=F32)
        return ((dot(high) + dot(mid)) + dot(low))[:classes]

    make_tile(0, left0, 0, LANES)
    second.cross()
    right0.forward()
    make_tile(0, right0, LANES, LANES)
    sum_grad(0)
    inverse = Inverse(0)
    inverse.rough()
    grads[0].cross()
    second.gather()
    inverse.rough()
    inverse.rough()
    inverse.fine()
    inverse.fine()
    grads[0].gather()
    second.forward()
    inverse.polish()
    make_tile(1, second, 0, BLOCK)
    grads[0].finish()
    delta = make_delta(0, inverse.value)
    step = split_dot(delta, tiles[0], NT)
    padded[...] = padded[...] - step
    sum_grad(1)
    change[0] = step[:classes]
    change[1] = credit(0, delta)
    inverse = Inverse(1)
    inverse.rough()
    grads[1].cross()
    for each in spread:
        each.settle()
    grads[0].settle()
    inverse.rough()
    inverse.rough()
    inverse.fine()
    grads[1].gather()
    inverse.fine()
    inverse.polish()
    grads[1].finish()
    delta = make_delta(1, inverse.value)
    change[0] = change[0] + split_dot(delta, tiles[1], NT)[:classes]
    change[1] = change[1] + credit(1, delta)
    grads[1].settle()


def solution(mesh):
    n_group, n_dev = mesh.shape["group"], mesh.shape["dev"]
    layout = Layout(n_group, n_dev)

    def body(points, residual, coeffs, owners, offsets):
        features, here = points.shape
        classes = residual.shape[0]
        rows = -(-classes // SUB) * SUB
        half_share = layout.share(features // SUB)
        block_share = layout.share(features // SUB * HALVES)
        grads_share = layout.share(rows // SUB * HALVES)
        vmem = pl.BlockSpec(memory_space=pltpu.VMEM)
        outside = pl.BlockSpec(memory_space=pltpu.HBM)
        change = pl.pallas_call(
            functools.partial(kernel, layout, n_group),
            out_shape=jax.ShapeDtypeStruct((2,) + residual.shape, F32),
            in_specs=[outside] * 4,
            out_specs=vmem,
            scratch_shapes=[
                pltpu.SMEM(owners.shape, jnp.int32),
                pltpu.SMEM(offsets.shape, jnp.int32),
                pltpu.VMEM(points.shape, F32),
                pltpu.VMEM(residual.shape, F32),
                pltpu.VMEM((rows, here), F32),
                pltpu.VMEM((2, here, features), jnp.bfloat16),
                pltpu.VMEM((2, here, BLOCK), F32),
                pltpu.SemaphoreType.DMA((4,)),
            ]
            + sum_scratch(layout, half_share) * HALVES
            + sum_scratch(layout, block_share)
            + sum_scratch(layout, grads_share) * 2,
            compiler_params=pltpu.CompilerParams(
                collective_id=0, has_side_effects=True, vmem_limit_bytes=60 * 1024 * 1024
            ),
        )(owners, offsets, points, residual)
        return residual - change[0], coeffs + change[1]

    split = P(None, ("group", "dev"))
    return jax.shard_map(
        body,
        mesh=mesh,
        in_specs=(split, split, split, P(), P()),
        out_specs=(split, split),
        check_vma=False,
    )
```

```python
import functools

import jax
import jax.numpy as jnp
from jax import lax
from jax.experimental import pallas as pl
from jax.experimental.pallas import tpu as pltpu
from jax.sharding import PartitionSpec as P

BLOCK = 256
LANES = 128
HALVES = BLOCK // LANES
SUB = 8

ridge = 2.0
step_norm = 1.5

MESH = pl.DeviceIdType.MESH
F32 = jnp.float32


def exact_dot(a, b, dims):
    return lax.dot_general(
        a, b, (dims, ((), ())), precision=lax.Precision.HIGHEST, preferred_element_type=F32
    )


NN = ((1,), (0,))
NT = ((1,), (1,))


def low_dot(a, b):
    return jnp.dot(a.astype(jnp.bfloat16), b.astype(jnp.bfloat16), preferred_element_type=F32)


def split_dot(a, b, dims=NN):
    ah, bh = a.astype(jnp.bfloat16), b.astype(jnp.bfloat16)
    al = (a - ah.astype(F32)).astype(jnp.bfloat16)
    bl = (b - bh.astype(F32)).astype(jnp.bfloat16)
    dot = lambda u, v: lax.dot_general(u, v, (dims, ((), ())), preferred_element_type=F32)
    return dot(ah, bh) + (dot(ah, bl) + dot(al, bh))


def split_two(x):
    high = x.astype(jnp.bfloat16)
    return high, (x - high.astype(F32)).astype(jnp.bfloat16)


def joined(parts):
    return parts[0].astype(F32) + parts[1].astype(F32)


def cross_dot(left, right):
    width = right[0].shape[1]
    both = jnp.concatenate(right, axis=1)
    out = jnp.dot(left[0], both, preferred_element_type=F32)
    out = out + jnp.dot(left[1], both, preferred_element_type=F32)
    return out[:, :width] + out[:, width:]


def split_three(x):
    high = x.astype(jnp.bfloat16)
    rest = x - high.astype(F32)
    mid = rest.astype(jnp.bfloat16)
    return high, mid, (rest - mid.astype(F32)).astype(jnp.bfloat16)


def line_width(n_dev):
    width = 1
    while n_dev % (2 * width) == 0 and 4 * width * width <= n_dev:
        width *= 2
    return width


class Layout:
    def __init__(self, n_group, n_dev):
        self.n_dev = n_dev
        self.width = line_width(n_dev)
        self.plane = n_group * self.width
        self.line = n_dev // self.width
        self.cores = 2 if n_group % 2 == 0 else 1
        self.chips = self.plane // self.cores

    def share(self, tiles):
        return -(-tiles // self.plane)


class Sum:
    def __init__(self, layout, at, share, refs):
        self.layout, self.share = layout, share
        self.group, self.dev = at
        self.terms, self.landed, self.held, self.crossed, self.total, self.sems = refs
        self.place = self.group * layout.width + lax.rem(self.dev, layout.width)
        self.plane = self.dev // layout.width
        self.sent = {}

    def peer_in_plane(self, k):
        to = lax.rem(self.place + k, self.layout.plane)
        width = self.layout.width
        return to, (to // width, self.plane * width + lax.rem(to, width))

    def peer_in_line(self, k):
        to = lax.rem(self.plane + k, self.layout.line)
        width = self.layout.width
        return self.group, to * width + lax.rem(self.dev, width)

    def piece(self, index):
        return pl.ds(index * self.share, self.share)

    def send(self, src, dst, to, out_sem, in_sem, pieces=1):
        pltpu.make_async_remote_copy(
            src_ref=src,
            dst_ref=dst,
            send_sem=self.sems.at[0, out_sem],
            recv_sem=self.sems.at[1, in_sem],
            device_id=to,
            device_id_type=MESH,
        ).start()
        self.sent[out_sem] = self.sent.get(out_sem, 0) + pieces

    def wait(self, way, sem, count):
        if count:
            like = self.terms.at[pl.ds(0, count * self.share)]
            pltpu.make_async_copy(like, like, self.sems.at[way, sem]).wait()

    def scatter(self):
        for k in range(1, self.layout.plane):
            to, device = self.peer_in_plane(k)
            self.send(self.terms.at[self.piece(to)], self.landed.at[self.piece(k - 1)], device, 0, 0)

    def cross(self):
        self.wait(1, 0, self.layout.plane - 1)
        total = self.terms[self.piece(self.place)]
        for k in range(self.layout.plane - 1):
            total = total + self.landed[self.piece(k)]
        self.held[...] = total
        for k in range(1, self.layout.line):
            self.send(self.held, self.crossed.at[self.piece(k - 1)], self.peer_in_line(k), 1, 1)

    def gather(self):
        self.wait(1, 1, self.layout.line - 1)
        mine = self.total.at[self.piece(self.place)]
        total = self.held[...]
        for k in range(self.layout.line - 1):
            total = total + self.crossed[self.piece(k)]
        mine[...] = total
        for k in range(1, self.layout.plane):
            self.send(mine, mine, self.peer_in_plane(k)[1], 2, 2)

    def relay(self):
        pass

    def forward(self):
        pass

    def finish(self):
        self.wait(1, 2, self.layout.plane - 1)

    def settle(self):
        for sem, count in sorted(self.sent.items()):
            self.wait(0, sem, count)


class PairedSum(Sum):
    def __init__(self, *args):
        super().__init__(*args)
        layout = self.layout
        self.core = lax.rem(self.group, layout.cores)
        self.chip = (self.group // layout.cores) * layout.width + lax.rem(self.dev, layout.width)
        self.place = self.core * layout.chips + self.chip

    def sibling(self):
        return self.group + 1 - 2 * self.core, self.dev

    def other_chip(self, k):
        layout = self.layout
        to = lax.rem(self.chip + k, layout.chips)
        group = (to // layout.width) * layout.cores + self.core
        return to, (group, self.plane * layout.width + lax.rem(to, layout.width))

    def share_of(self, core):
        chips = self.layout.chips
        return pl.ds(core * chips * self.share, chips * self.share)

    def scatter(self):
        chips = self.layout.chips
        src, dst = self.terms.at[self.share_of(1 - self.core)], self.landed.at[: chips * self.share]
        self.send(src, dst, self.sibling(), 0, 0, chips)

    def relay(self):
        chips = self.layout.chips
        self.wait(1, 0, chips)
        mine = self.share_of(self.core)
        self.terms[mine] = self.terms[mine] + self.landed[: chips * self.share]
        for k in range(1, chips):
            to, device = self.other_chip(k)
            src = self.terms.at[self.piece(self.core * chips + to)]
            self.send(src, self.landed.at[self.piece(chips + k - 1)], device, 1, 1)

    def cross(self):
        layout, chips = self.layout, self.layout.chips
        self.wait(1, 1, chips - 1)
        total = self.terms[self.piece(self.place)]
        for k in range(1, chips):
            total = total + self.landed[self.piece(chips + k - 1)]
        self.held[...] = total
        for k in range(1, layout.line):
            self.send(self.held, self.crossed.at[self.piece(k - 1)], self.peer_in_line(k), 2, 2)

    def gather(self):
        layout, chips = self.layout, self.layout.chips
        self.wait(1, 2, layout.line - 1)
        total = self.held[...]
        for k in range(layout.line - 1):
            total = total + self.crossed[self.piece(k)]
        mine = self.total.at[self.piece(self.place)]
        mine[...] = total
        for k in range(1, chips):
            self.send(mine, mine, self.other_chip(k)[1], 3, 3)

    def forward(self):
        chips = self.layout.chips
        self.wait(1, 3, chips - 1)
        mine = self.total.at[self.share_of(self.core)]
        self.send(mine, mine, self.sibling(), 4, 4, chips)

    def finish(self):
        self.wait(1, 4, self.layout.chips)


def sum_scratch(layout, share):
    tile = (SUB, LANES)
    return [
        pltpu.VMEM((layout.plane * share,) + tile, F32),
        pltpu.VMEM((max(layout.plane - 1, 1) * share,) + tile, F32),
        pltpu.VMEM((share,) + tile, F32),
        pltpu.VMEM((max(layout.line - 1, 1) * share,) + tile, F32),
        pltpu.VMEM((layout.plane * share,) + tile, F32),
        pltpu.SemaphoreType.DMA((2, 5)),
    ]


def to_tiles(ref, value):
    rows, columns = value.shape
    half = rows // SUB
    for c in range(columns // LANES):
        ref[c * half : (c + 1) * half] = value[:, c * LANES : (c + 1) * LANES].reshape(half, SUB, LANES)
    left = ref.shape[0] - half * (columns // LANES)
    if left:
        ref[ref.shape[0] - left :] = jnp.zeros((left, SUB, LANES), F32)


def from_tiles(ref, rows, columns):
    half = rows // SUB
    return jnp.concatenate(
        [ref[c * half : (c + 1) * half].reshape(rows, LANES) for c in range(columns // LANES)], axis=1
    )


def kernel(layout, n_group, owners_in, offsets_in, points_in, residual_in, change, *scratch):
    owners, offsets, points, residual, padded, flipped, tiles, loads = scratch[:8]
    sums = [scratch[8 + 6 * i : 14 + 6 * i] for i in range(2 * HALVES + 2)]
    group, dev = lax.axis_index("group"), lax.axis_index("dev")
    me = group * layout.n_dev + dev
    features, here_points = points.shape
    classes = residual.shape[0]
    rows = padded.shape[0]

    copies = [
        pltpu.make_async_copy(src, dst, loads.at[i])
        for i, (src, dst) in enumerate(
            [(points_in, points), (owners_in, owners), (offsets_in, offsets), (residual_in, residual)]
        )
    ]
    for copy in copies:
        copy.start()

    blocks_share = sums[0][2].shape[0]
    grads_share = sums[-1][2].shape[0]
    BlockSum = PairedSum if layout.cores == 2 else Sum
    at = (group, dev)
    spread = [BlockSum(layout, at, blocks_share, refs) for refs in sums[: 2 * HALVES]]
    grads = [Sum(layout, at, grads_share, refs) for refs in sums[2 * HALVES :]]
    left0, right0, left1, right1 = spread

    barrier = pltpu.get_barrier_semaphore()
    peers = [grads[0].peer_in_plane(k)[1] for k in range(1, layout.plane)]
    peers += [grads[0].peer_in_line(k) for k in range(1, layout.line)]
    for peer in peers:
        pl.semaphore_signal(barrier, inc=1, device_id=peer, device_id_type=MESH)

    def picker(step):
        first = jnp.where(owners[step] == me, offsets[step], 4 * here_points)
        row = lax.broadcasted_iota(jnp.int32, (BLOCK, here_points), 0)
        col = lax.broadcasted_iota(jnp.int32, (BLOCK, here_points), 1)
        return jnp.where(col == row + first, 1.0, 0.0).astype(jnp.bfloat16)

    def pick(index):
        chosen = picker(index // HALVES)
        at = index % HALVES * LANES
        chosen = chosen[at : at + LANES]
        dot = lambda a: lax.dot_general(a, chosen, (NT, ((), ())), preferred_element_type=F32)
        high, mid, low = pieces
        to_tiles(spread[index].terms, (dot(high) + dot(mid)) + dot(low))

    for copy in copies[:3]:
        copy.wait()
    pieces = split_three(points[...])
    pick(0)
    pl.semaphore_wait(barrier, len(peers))
    left0.scatter()
    pick(1)
    left0.relay()
    right0.scatter()
    cols = split_two(points[...].T)
    flipped[0], flipped[1] = cols
    right0.relay()
    left0.cross()
    cols = joined(cols)
    cols_norm = jnp.sum(cols * cols, axis=1, keepdims=True)
    right0.cross()
    pick(2)
    left1.scatter()
    for copy in copies[3:]:
        copy.wait()
    padded[...] = jnp.zeros_like(padded)
    padded[:classes] = residual[...]
    left0.gather()
    left1.relay()
    pick(3)
    right1.scatter()
    right0.gather()
    left1.cross()
    left0.forward()
    right1.relay()

    eye = (
        lax.broadcasted_iota(jnp.int32, (BLOCK, BLOCK), 0)
        == lax.broadcasted_iota(jnp.int32, (BLOCK, BLOCK), 1)
    ).astype(F32)

    def kernel_tile(left, left_norm, right):
        right = split_two(right)
        whole = joined(right)
        right_norm = jnp.sum(whole * whole, axis=0, keepdims=True)
        return jnp.exp(-(left_norm + right_norm - 2.0 * cross_dot(left, right)) / features)

    def half_block(index):
        return from_tiles(spread[index].total, features, LANES)

    def half_tile(index):
        spread[index].finish()
        at = index % HALVES * LANES
        tiles[index // HALVES, :, at : at + LANES] = kernel_tile(
            (flipped[0], flipped[1]), cols_norm, half_block(index)
        )

    class Inverse:
        def __init__(self, step):
            halves = [half_block(HALVES * step + h) for h in range(HALVES)]
            b = jnp.concatenate(halves, axis=1)
            rows = split_two(b.T)
            whole = joined(rows)
            gram = kernel_tile(rows, jnp.sum(whole * whole, axis=1, keepdims=True), b) + ridge * eye
            top = jnp.max(jnp.sum(gram, axis=1, keepdims=True), axis=0, keepdims=True)
            centre = 2.0 / (ridge + top)
            err = (top - ridge) / (top + ridge)
            gain = 2.0 / (2.0 - err * err)
            self.gram = gram
            self.value = (gain * centre) * (2.0 * eye - centre * gram)
            self.err = err * err / (2.0 - err * err)

        def gain(self):
            err = self.err
            self.err = err * err / (2.0 - err * err)
            return 2.0 / (2.0 - err * err)

        def rough(self):
            near = self.value.astype(jnp.bfloat16)
            rest = eye - low_dot(self.gram, near)
            self.value = self.gain() * (near.astype(F32) + low_dot(near, rest))

        def fine(self):
            rest = eye - split_dot(self.gram, self.value)
            self.value = self.gain() * (self.value + low_dot(self.value, rest))

        def polish(self):
            rest = eye - exact_dot(self.gram, self.value, NN)
            self.value = self.value + low_dot(self.value, rest)

    def sum_grad(step):
        to_tiles(grads[step].terms, exact_dot(padded[...], tiles[step], NN))
        grads[step].scatter()

    def make_delta(step, inverse):
        grad = from_tiles(grads[step].total, rows, BLOCK)
        square = jnp.sum(jnp.sum(grad * grad, axis=1, keepdims=True), axis=0, keepdims=True)
        scale = step_norm / jnp.sqrt(square / (classes * BLOCK) + 1e-06)
        return scale * exact_dot(grad, inverse, NN)

    def credit(step, delta):
        chosen = picker(step)
        high, mid, low = split_three(delta)
        dot = lambda a: jnp.dot(a, chosen, preferred_element_type=F32)
        return ((dot(high) + dot(mid)) + dot(low))[:classes]

    half_tile(0)
    right0.forward()
    right1.cross()
    half_tile(1)
    sum_grad(0)
    inverse = Inverse(0)
    inverse.rough()
    grads[0].cross()
    left1.gather()
    right1.gather()
    inverse.rough()
    inverse.rough()
    inverse.fine()
    inverse.fine()
    grads[0].gather()
    left1.forward()
    right1.forward()
    half_tile(2)
    half_tile(3)
    inverse.polish()
    grads[0].finish()
    delta = make_delta(0, inverse.value)
    step = split_dot(delta, tiles[0], NT)
    padded[...] = padded[...] - step
    sum_grad(1)
    change[0] = step[:classes]
    change[1] = credit(0, delta)
    inverse = Inverse(1)
    inverse.rough()
    grads[1].cross()
    for each in spread:
        each.settle()
    grads[0].settle()
    inverse.rough()
    inverse.rough()
    inverse.fine()
    grads[1].gather()
    inverse.fine()
    inverse.polish()
    grads[1].finish()
    delta = make_delta(1, inverse.value)
    change[0] = change[0] + split_dot(delta, tiles[1], NT)[:classes]
    change[1] = change[1] + credit(1, delta)
    grads[1].settle()


def solution(mesh):
    n_group, n_dev = mesh.shape["group"], mesh.shape["dev"]
    layout = Layout(n_group, n_dev)

    def body(points, residual, coeffs, owners, offsets):
        features, here = points.shape
        classes = residual.shape[0]
        rows = -(-classes // SUB) * SUB
        blocks_share = layout.share(features // SUB)
        grads_share = layout.share(rows // SUB * HALVES)
        vmem = pl.BlockSpec(memory_space=pltpu.VMEM)
        outside = pl.BlockSpec(memory_space=pltpu.HBM)
        change = pl.pallas_call(
            functools.partial(kernel, layout, n_group),
            out_shape=jax.ShapeDtypeStruct((2,) + residual.shape, F32),
            in_specs=[outside] * 4,
            out_specs=vmem,
            scratch_shapes=[
                pltpu.SMEM(owners.shape, jnp.int32),
                pltpu.SMEM(offsets.shape, jnp.int32),
                pltpu.VMEM(points.shape, F32),
                pltpu.VMEM(residual.shape, F32),
                pltpu.VMEM((rows, here), F32),
                pltpu.VMEM((2, here, features), jnp.bfloat16),
                pltpu.VMEM((2, here, BLOCK), F32),
                pltpu.SemaphoreType.DMA((4,)),
            ]
            + sum_scratch(layout, blocks_share) * (2 * HALVES)
            + sum_scratch(layout, grads_share) * 2,
            compiler_params=pltpu.CompilerParams(
                collective_id=0, has_side_effects=True, vmem_limit_bytes=60 * 1024 * 1024
            ),
        )(owners, offsets, points, residual)
        return residual - change[0], coeffs + change[1]

    split = P(None, ("group", "dev"))
    return jax.shard_map(
        body,
        mesh=mesh,
        in_specs=(split, split, split, P(), P()),
        out_specs=(split, split),
        check_vma=False,
    )
```
